128 devices in a mesh: section: 2 (over y_hi), dp: 64 (over x, y_lo, z, core).
Axes of the slice: x: 4, y: 4 (y_hi: 2, y_lo: 2; y = y_hi * 2 + y_lo), z: 4, core: 2. Of those that a mesh axis runs over, the one named last changes fastest.
Arguments:
- block_input: bfloat16 [4, 2048, 2048], P(None, 'dp'), may hold values from -16 to 16
- segment_ids: int32 [4, 2048], P(None, 'dp'), may hold values from 0 to 31, as said below
- cotangent: bfloat16 [4, 2048, 2048], P(None, 'dp'), may hold values from -16 to 16
- first_gain: bfloat16 [2, 2048], P('section', 'dp'), may hold values from 0.25 to 1.75
- first_shift: bfloat16 [2, 2048], P('section', 'dp'), may hold values from -3 to 3
- qkv_weight: bfloat16 [2, 2048, 6144], P('section', 'dp'), may hold values from -0.125 to 0.125
- qkv_bias: bfloat16 [2, 6144], P('section', 'dp'), may hold values from -3 to 3
- out_weight: bfloat16 [2, 2048, 2048], P('section', 'dp'), may hold values from -0.25 to 0.25
- second_gain: bfloat16 [2, 2048], P('section', 'dp'), may hold values from 0.25 to 1.75
- second_shift: bfloat16 [2, 2048], P('section', 'dp'), may hold values from -3 to 3
- gate_up: bfloat16 [2, 2048, 11264], P('section', 'dp'), may hold values from -0.125 to 0.125
- down_weight: bfloat16 [2, 5632, 2048], P('section', 'dp'), may hold values from -0.078125 to 0.078125
Outputs:
- activations: bfloat16 [2, 4, 2048, 2048], P('section', None, 'dp')
- input_grads: float32 [2, 4, 2048, 2048], P('section', None, 'dp')
- first_gain_grad: float32 [2, 2048], P('section', 'dp')
- first_shift_grad: float32 [2, 2048], P('section', 'dp')
- qkv_weight_grad: float32 [2, 2048, 6144], P('section', 'dp')
- qkv_bias_grad: float32 [2, 6144], P('section', 'dp')
- out_weight_grad: float32 [2, 2048, 2048], P('section', 'dp')
- second_gain_grad: float32 [2, 2048], P('section', 'dp')
- second_shift_grad: float32 [2, 2048], P('section', 'dp')
- gate_up_grad: float32 [2, 2048, 11264], P('section', 'dp')
- down_weight_grad: float32 [2, 5632, 2048], P('section', 'dp')
The draws below stay inside these ranges and needn't reach their ends.
Inputs may be any that keep to these rules, and one draw needn't show every extreme that they name: `segment_ids`: within each aligned block of 32 rows (one dp index of one micro-batch) the ids start at 0 and rise by 0 or 1 from row to row, so each sequence is a run of rows; in some block one sequence fills all 32 rows, in another every row is a sequence of its own.
All inputs are finite; a program needn't handle non-finite values.
Results may differ from the reference program's by a relative error of at most 0.017.
Values may be sent and summed in bfloat16 or wider, within the bound.
No kernel may reach another device: no remote copies, remote signals or barrier semaphores. Data moves between devices by JAX's collectives and lax.ppermute only.
A program may use at most 576 MiB of HBM per device.

```python
import jax
import jax.numpy as jnp
from jax import lax

D = 2048
HEADS = 32
HEAD_DIM = 64
ROT = 16
FF = 5632
MICRO = 4
ROWS = 32
TOKENS = 2048
N_SECTION = 2
N_DP = 64


def draw_segment_ids(key, part):
    key = jax.random.fold_in(key, 7)
    blocks = MICRO * TOKENS // ROWS
    starts = jax.random.randint(jax.random.fold_in(key, 1), (blocks, ROWS), 0, 24) == 0
    whole_block = jax.random.randint(jax.random.fold_in(key, 2), (), 0, blocks)
    offset = jax.random.randint(jax.random.fold_in(key, 3), (), 1, blocks)
    single_block = (whole_block + offset) % blocks
    block_index = jnp.arange(blocks, dtype=jnp.int32)[:, None]
    row_index = jnp.arange(ROWS, dtype=jnp.int32)[None, :]
    starts = jnp.where(block_index == single_block, True, starts)
    starts = jnp.where(block_index == whole_block, False, starts)
    starts = jnp.where(row_index == 0, False, starts)
    return jnp.cumsum(starts.astype(jnp.int32), axis=1).reshape(MICRO, TOKENS)


def with_spikes(values, own_key, source, target, blocks, factor):
    def block_of(dim):
        return (jnp.arange(values.shape[dim]) // (values.shape[dim] // blocks)).reshape((-1,) + (1,) * (values.ndim - 1 - dim))

    first = jax.random.permutation(own_key, blocks)[block_of(target)]
    other_side = (block_of(target) + blocks // 2) % blocks
    return jnp.where((block_of(source) == first) | (block_of(source) == other_side), factor * values, values)


def levels(key, dims, cuts, least, high):
    def one(dim, parts):
        heights = jax.random.uniform(jax.random.fold_in(jax.random.fold_in(key, 6), dim), (parts,), jnp.float32, least / len(cuts), high / len(cuts))
        return jnp.repeat(jnp.exp(heights), dims[dim] // parts).reshape((-1,) + (1,) * (len(dims) - dim - 1))

    level = one(*cuts[0])
    for cut in cuts[1:]:
        level = level * one(*cut)
    return level


def normal_values(own_key, extent, width, reach, split=(), kind=jnp.bfloat16):
    entries = jax.random.normal(own_key, extent, jnp.float32) * width
    if len(split) > 0:
        entries = levels(own_key, extent, split, -0.22, 0.18) * entries
    return jnp.clip(entries, min=-reach, max=reach).astype(kind)


def noise_with(stream_key, extent, scale, reach, cuts, heavy, kind=jnp.bfloat16):
    result = scale * jax.random.normal(stream_key, extent, jnp.float32)
    if cuts:
        result = result * levels(stream_key, extent, cuts, -0.22, 0.18)
    return jnp.clip(with_spikes(result, jax.random.fold_in(stream_key, 3), *heavy), -reach, reach).astype(kind)


def setup_inputs(seed: int = 0) -> dict:
    splits = jax.random.split(jax.random.key(seed), 13)
    block_input = noise_with(splits[0], (MICRO, TOKENS, D), 1.0, 16.0, ((1, 64),), (1, 2, 64, 4.0))
    segment_ids = draw_segment_ids(jax.random.fold_in(splits[12], 71), 0)
    cotangent = noise_with(splits[2], (MICRO, TOKENS, D), 1.0, 16.0, ((1, 64),), (1, 2, 64, 4.0))
    first_gain = jnp.clip(1.0 + 0.15 * jax.random.normal(splits[3], (N_SECTION, D), jnp.float32), 0.25, 1.75).astype(jnp.bfloat16)
    first_shift = normal_values(splits[4], (N_SECTION, D), 0.5, 3.0, ((0, 2), (1, 64)))
    qkv_weight = normal_values(splits[5], (N_SECTION, D, 3 * D), D ** -0.5, 0.125, ((0, 2), (1, 64)))
    qkv_bias = normal_values(splits[6], (N_SECTION, 3 * D), 0.5, 3.0, ((0, 2), (1, 64)))
    out_weight = normal_values(splits[7], (N_SECTION, D, D), (D // 4) ** -0.5, 0.25, ((0, 2), (1, 64)))
    second_gain = jnp.clip(1.0 + 0.15 * jax.random.normal(splits[8], (N_SECTION, D), jnp.float32), 0.25, 1.75).astype(jnp.bfloat16)
    second_shift = normal_values(splits[9], (N_SECTION, D), 0.5, 3.0, ((0, 2), (1, 64)))
    gate_up = normal_values(splits[10], (N_SECTION, D, 2 * FF), D ** -0.5, 0.125, ((0, 2), (1, 64)))
    down_weight = normal_values(splits[11], (N_SECTION, FF, D), FF ** -0.5, 0.078125, ((0, 2), (1, 64)))
    return dict(block_input=block_input, segment_ids=segment_ids, cotangent=cotangent, first_gain=first_gain, first_shift=first_shift, qkv_weight=qkv_weight, qkv_bias=qkv_bias, out_weight=out_weight, second_gain=second_gain, second_shift=second_shift, gate_up=gate_up, down_weight=down_weight)


EPSILON = 1e-05
NEG_FILL = -1e+30

@jax.custom_vjp
def low(v):
    return lax.optimization_barrier(v.astype(jnp.bfloat16)).astype(jnp.float32)

@jax.custom_vjp
def low_back(v):
    return v

def low_keep(v):
    return (low(v), None)

def low_pass(kept, grad):
    return (grad,)

def back_keep(v):
    return (v, None)

def back_low(kept, grad):
    return (low(grad),)
low.defvjp(low_keep, low_pass)
low_back.defvjp(back_keep, back_low)

def product(left, right):
    return jnp.einsum('brd,df->brf', left, right, precision=lax.Precision.HIGHEST)

def normalize(values, gain, shift):
    mean = lax.optimization_barrier(jnp.mean(values, axis=-1, keepdims=True))
    centred = values - mean
    return centred * lax.rsqrt(lax.optimization_barrier(jnp.mean(centred * centred, axis=-1, keepdims=True)) + EPSILON) * gain + shift

def geometry(segments):
    count = segments.shape[-1]
    index = jnp.arange(count, dtype=jnp.int32)
    same = segments[..., :, None] == segments[..., None, :]
    before = index[None, :] < index[:, None]
    places = lax.optimization_barrier(jnp.sum(jnp.where(same & before, 1.0, 0.0), axis=-1)).astype(jnp.float32)
    inverse = 10000.0 ** (-(jnp.arange(ROT // 2).astype(jnp.float32) * 2.0 / ROT))
    theta = places[..., None] * inverse
    allowed = same & (index[None, :] <= index[:, None])
    return (jnp.cos(theta)[..., None, :], jnp.sin(theta)[..., None, :], allowed)

def turn(values, cosine, sine):
    half = ROT // 2
    first = values[..., :half]
    second = values[..., half:ROT]
    return jnp.concatenate([first * cosine - second * sine, second * cosine + first * sine, values[..., ROT:]], axis=-1)

def layer(inputs, weights, cosine, sine, allowed):
    first_gain, first_shift, qkv_weight, qkv_bias, out_weight, second_gain, second_shift, gate_up, down_weight = weights
    blocks, rows = (inputs.shape[0], inputs.shape[1])
    normed = low(normalize(inputs, first_gain, first_shift))
    projected = low_back(product(normed, qkv_weight) + qkv_bias).reshape(blocks, rows, 3, HEADS, HEAD_DIM)
    queries = low(turn(projected[:, :, 0], cosine, sine))
    key_rows = low(turn(projected[:, :, 1], cosine, sine))
    value_rows = low(projected[:, :, 2])
    scores = low_back(jnp.einsum('bqhd,bkhd->bhqk', queries, key_rows, precision=lax.Precision.HIGHEST) * HEAD_DIM ** (-0.5))
    scores = jnp.where(allowed[:, None], scores, NEG_FILL)
    top = lax.optimization_barrier(jnp.max(scores, axis=-1, keepdims=True))
    spread = jnp.exp(scores - top)
    probs = spread / lax.optimization_barrier(jnp.sum(spread, axis=-1, keepdims=True))
    mixed = jnp.einsum('bhqk,bkhd->bqhd', low(probs), value_rows, precision=lax.Precision.HIGHEST)
    mixed = low(low_back(mixed.reshape(blocks, rows, HEADS * HEAD_DIM)))
    hidden = inputs + low_back(product(mixed, out_weight))
    normed_two = low(normalize(hidden, second_gain, second_shift))
    gate_up_out = low_back(product(normed_two, gate_up))
    gate_part = gate_up_out[..., :FF]
    activated = low(gate_part * jax.nn.sigmoid(gate_part) * gate_up_out[..., FF:])
    return hidden + low_back(product(activated, down_weight))

def reference(block_input, segment_ids, cotangent, first_gain, first_shift, qkv_weight, qkv_bias, out_weight, second_gain, second_shift, gate_up, down_weight):
    weights = tuple((item.astype(jnp.float32) for item in (first_gain, first_shift, qkv_weight, qkv_bias, out_weight, second_gain, second_shift, gate_up, down_weight)))
    inputs = block_input.astype(jnp.float32).reshape(MICRO, N_DP, ROWS, D)
    segments = segment_ids.reshape(MICRO, N_DP, ROWS)
    upstream = cotangent.astype(jnp.float32).reshape(MICRO, N_DP, ROWS, D)
    probe = jnp.zeros_like(inputs)

    def forward(inputs, probe, weights):

        def pair(pieces):
            rows_in, probe_rows, segs = pieces
            cosine, sine, allowed = geometry(segs)
            first = layer(rows_in, tuple((item[0] for item in weights)), cosine, sine, allowed)
            passed = low(low_back(first + probe_rows))
            second = layer(passed, tuple((item[1] for item in weights)), cosine, sine, allowed)
            return (first, second)
        return lax.map(jax.checkpoint(pair), (inputs, probe, segments))
    outputs, pullback = jax.vjp(forward, inputs, probe, weights)
    first, second = outputs
    grad_inputs, grad_probe, grad_weights = pullback((jnp.zeros_like(first), upstream))
    activations = jnp.stack([first, second]).reshape(2, MICRO, TOKENS, D).astype(jnp.bfloat16)
    input_grads = jnp.stack([grad_inputs, grad_probe]).reshape(2, MICRO, TOKENS, D)
    return (activations, input_grads, grad_weights[0], grad_weights[1], grad_weights[2], grad_weights[3], grad_weights[4], grad_weights[5], grad_weights[6], grad_weights[7], grad_weights[8])
```

```python
import functools
import math

import jax
import jax.numpy as jnp
from jax import lax
from jax.experimental import pallas as pl
from jax.experimental.pallas import tpu as pltpu
from jax.sharding import Mesh
from jax.sharding import PartitionSpec as P

D = 2048
HEAD_DIM = 64
ROT = 16
FF = 5632
EPSILON = 1e-05
NEG_FILL = -1e30
TILE = 256
BLOCKS = D // TILE
ROWS = 64
GROUP = 8 * ROWS
HALF = GROUP // 2
LOCAL = 704
PIECE = 88
PADDED = 96
WIDE = 8 * PADDED
ATTN = 4 * TILE
MLP = 9 * TILE
VEC = 16
VMEM = 56 * 1024 * 1024
F32 = jnp.float32
BF16 = jnp.bfloat16

GRID = ("section", "x", "y", "z", "core")
DP = ("x", "y", "z", "core")
RING = ("section", "y")
SPREAD = ("section", "y", "z")


def dot(a, b):
    return jnp.dot(a, b, preferred_element_type=F32)


def dot_nt(a, b):
    return lax.dot_general(a, b, (((1,), (1,)), ((), ())), preferred_element_type=F32)


def dot_tn(a, b):
    return lax.dot_general(a, b, (((0,), (0,)), ((), ())), preferred_element_type=F32)


def call(kernel, outs, in_specs, *args, flops):
    moved = sum(math.prod(o.shape) * o.dtype.itemsize for o in outs) + 8 * 1024 * 1024
    return pl.pallas_call(
        kernel,
        grid=(1,),
        in_specs=in_specs,
        out_specs=[whole(o.shape) for o in outs],
        out_shape=outs,
        compiler_params=pltpu.CompilerParams(vmem_limit_bytes=VMEM),
        cost_estimate=pl.CostEstimate(flops=flops, bytes_accessed=moved, transcendentals=0),
    )(*args)


def whole(shape):
    return pl.BlockSpec(shape, lambda i: (0,) * len(shape), pipeline_mode=pl.Buffered(1))


def of_layer(layer, rows):
    return pl.BlockSpec(
        (1, BLOCKS, rows, TILE), lambda i: (layer, 0, 0, 0), pipeline_mode=pl.Buffered(1)
    )


def shape_of(*dims, dtype=BF16):
    return jax.ShapeDtypeStruct(dims, dtype)


def both(a_ref, b_ref):
    return jnp.concatenate([a_ref[...], b_ref[...]], axis=0)


def tile_of(w_ref, row, count=TILE):
    return w_ref[0, :, row : row + count, :].reshape(BLOCKS * count, TILE)


def twisted(u, table_ref, sign):
    def wide(k):
        t = table_ref[k]
        return jnp.concatenate([t, t], axis=1)

    n = u.shape[1]
    half = ROT // 2
    side = pltpu.roll(u, n - half, 1) * wide(1) + pltpu.roll(u, half, 1) * wide(2)
    return u * wide(0) + (side if sign > 0 else -side)


def pair_mask(h):
    lane = lax.broadcasted_iota(jnp.int32, (128, 128), 1)
    return (lane // HEAD_DIM) == h


def value_mask(h):
    lane = lax.broadcasted_iota(jnp.int32, (128, TILE), 1)
    return (lane // 32) % 4 == h


def probabilities(q, k, g, h, mask_ref):
    rows = slice(128 * g, 128 * g + 128)
    lanes = slice(128 * (h // 2), 128 * (h // 2) + 128)
    qh = jnp.where(pair_mask(h % 2), q[rows, lanes], jnp.zeros((), BF16))
    s = dot_nt(qh, k[rows, lanes]) * HEAD_DIM**-0.5
    m = mask_ref[rows, :]
    s = jnp.where(m > 0, s, NEG_FILL)
    e = jnp.exp(s - jnp.max(s, axis=1, keepdims=True))
    return e / jnp.sum(e, axis=1, keepdims=True)


def attention_kernel(na_ref, nb_ref, w_ref, bias_ref, table_ref, mask_ref, pa_ref, pb_ref, q_ref, k_ref, v_ref, o_ref):
    n = both(na_ref, nb_ref)
    for j, ref in enumerate((q_ref, k_ref, v_ref)):
        u = dot(n, tile_of(w_ref, TILE * j)) + bias_ref[j : j + 1, :]
        ref[...] = (twisted(u, table_ref, 1) if j < 2 else u).astype(BF16)
    q, k, v = q_ref[...], k_ref[...], v_ref[...]
    for g in range(GROUP // 128):
        rows = slice(128 * g, 128 * g + 128)
        o = jnp.zeros((128, TILE), F32)
        for h in range(4):
            p = probabilities(q, k, g, h, mask_ref).astype(BF16)
            o = jnp.where(value_mask(h), dot(p, v[rows]), o)
        o_ref[rows, :] = o.astype(BF16)
    o = o_ref[...]
    for j in range(BLOCKS):
        part = dot(o, tile_of(w_ref, 3 * TILE + 32 * j, 32)).astype(BF16)
        pa_ref[:, TILE * j : TILE * (j + 1)] = part[:HALF]
        pb_ref[:, TILE * j : TILE * (j + 1)] = part[HALF:]


def attention(layer, na, nb, weights, bias, table, mask):
    return call(
        attention_kernel,
        [shape_of(HALF, D), shape_of(HALF, D)] + [shape_of(GROUP, TILE)] * 4,
        [whole(na.shape), whole(nb.shape), of_layer(layer, ATTN), whole(bias.shape), whole(table.shape), whole(mask.shape)],
        na, nb, weights, bias, table, mask,
        flops=2 * GROUP * D * ATTN,
    )


def feed_kernel(na_ref, nb_ref, w_ref, pa_ref, pb_ref, g_ref, u_ref, act_ref):
    n = both(na_ref, nb_ref)
    for j in range(3):
        lanes = slice(TILE * j, TILE * (j + 1))
        g = dot(n, tile_of(w_ref, TILE * j))
        u = dot(n, tile_of(w_ref, TILE * (3 + j)))
        g_ref[:, lanes] = g
        u_ref[:, lanes] = u
        act_ref[:, lanes] = (g * jax.nn.sigmoid(g) * u).astype(BF16)
    act = act_ref[...]
    for j in range(BLOCKS):
        part = dot(act, tile_of(w_ref, 6 * TILE + PADDED * j, PADDED)).astype(BF16)
        pa_ref[:, TILE * j : TILE * (j + 1)] = part[:HALF]
        pb_ref[:, TILE * j : TILE * (j + 1)] = part[HALF:]


def feed(layer, na, nb, weights):
    return call(
        feed_kernel,
        [shape_of(HALF, D), shape_of(HALF, D), shape_of(GROUP, WIDE, dtype=F32), shape_of(GROUP, WIDE, dtype=F32), shape_of(GROUP, WIDE)],
        [whole(na.shape), whole(nb.shape), of_layer(layer, MLP)],
        na, nb, weights,
        flops=2 * GROUP * D * MLP,
    )


def feed_back_kernel(ma_ref, mb_ref, w_ref, g_ref, u_ref, ea_ref, eb_ref, dg_ref, du_ref):
    gm = both(ma_ref, mb_ref)
    da = jnp.zeros((GROUP, WIDE), F32)
    for j in range(BLOCKS):
        da += dot_nt(gm[:, TILE * j : TILE * (j + 1)], tile_of(w_ref, 6 * TILE + PADDED * j, PADDED))
    g = g_ref[...]
    u = u_ref[...]
    sigma = jax.nn.sigmoid(g)
    dg_ref[...] = (da * u * sigma * (1.0 + g * (1.0 - sigma))).astype(BF16)
    du_ref[...] = (da * g * sigma).astype(BF16)
    dg = dg_ref[...]
    du = du_ref[...]
    for b in range(BLOCKS):
        e = jnp.zeros((GROUP, TILE), F32)
        for j in range(3):
            lanes = slice(TILE * j, TILE * (j + 1))
            e += dot_nt(dg[:, lanes], w_ref[0, b, TILE * j : TILE * (j + 1), :])
            e += dot_nt(du[:, lanes], w_ref[0, b, TILE * (3 + j) : TILE * (4 + j), :])
        e = e.astype(BF16)
        ea_ref[:, TILE * b : TILE * (b + 1)] = e[:HALF]
        eb_ref[:, TILE * b : TILE * (b + 1)] = e[HALF:]


def feed_back(layer, ma, mb, weights, g, u):
    return call(
        feed_back_kernel,
        [shape_of(HALF, D), shape_of(HALF, D), shape_of(GROUP, WIDE), shape_of(GROUP, WIDE)],
        [whole(ma.shape), whole(mb.shape), of_layer(layer, MLP), whole(g.shape), whole(u.shape)],
        ma, mb, weights, g, u,
        flops=2 * GROUP * D * MLP,
    )


def attention_back_kernel(
    da_ref, db_ref, w_ref, q_ref, k_ref, v_ref, table_ref, mask_ref, ea_ref, eb_ref, dq_ref, dk_ref, dv_ref, db_sum_ref
):
    dattn = both(da_ref, db_ref)
    do = jnp.zeros((GROUP, TILE), F32)
    for j in range(BLOCKS):
        do += dot_nt(dattn[:, TILE * j : TILE * (j + 1)], tile_of(w_ref, 3 * TILE + 32 * j, 32))
    do = do.astype(BF16)
    q, k, v = q_ref[...], k_ref[...], v_ref[...]
    dqs, dks = [], []
    for g in range(GROUP // 128):
        rows = slice(128 * g, 128 * g + 128)
        dv = jnp.zeros((128, TILE), F32)
        dq_pairs, dk_pairs = [], []
        for pair in range(2):
            lanes = slice(128 * pair, 128 * pair + 128)
            dq = jnp.zeros((128, 128), F32)
            dk = jnp.zeros((128, 128), F32)
            for h in (2 * pair, 2 * pair + 1):
                p = probabilities(q, k, g, h, mask_ref)
                doh = jnp.where(value_mask(h), do[rows], jnp.zeros((), BF16))
                dp = dot_nt(doh, v[rows])
                ds = p * (dp - jnp.sum(p * dp, axis=1, keepdims=True))
                ds = ds.astype(BF16)
                dv = jnp.where(value_mask(h), dot_tn(p.astype(BF16), do[rows]), dv)
                dq = jnp.where(pair_mask(h % 2), dot(ds, k[rows, lanes]), dq)
                dk = jnp.where(pair_mask(h % 2), dot_tn(ds, q[rows, lanes]), dk)
            dq_pairs.append(dq)
            dk_pairs.append(dk)
        dv_ref[rows, :] = dv.astype(BF16)
        dqs.append(jnp.concatenate(dq_pairs, axis=1))
        dks.append(jnp.concatenate(dk_pairs, axis=1))
    factor = HEAD_DIM**-0.5
    dq_ref[...] = twisted(jnp.concatenate(dqs, axis=0) * factor, table_ref, -1).astype(BF16)
    dk_ref[...] = twisted(jnp.concatenate(dks, axis=0) * factor, table_ref, -1).astype(BF16)
    parts = (dq_ref[...], dk_ref[...], dv_ref[...])
    db_sum_ref[...] = jnp.concatenate(
        [jnp.sum(part.astype(F32), axis=0, keepdims=True) for part in parts] + [jnp.zeros((5, TILE), F32)], axis=0
    )
    for b in range(BLOCKS):
        e = jnp.zeros((GROUP, TILE), F32)
        for j in range(3):
            e += dot_nt(parts[j], w_ref[0, b, TILE * j : TILE * (j + 1), :])
        e = e.astype(BF16)
        ea_ref[:, TILE * b : TILE * (b + 1)] = e[:HALF]
        eb_ref[:, TILE * b : TILE * (b + 1)] = e[HALF:]


def attention_back(layer, da, db, weights, q, k, v, table, mask):
    return call(
        attention_back_kernel,
        [shape_of(HALF, D), shape_of(HALF, D)] + [shape_of(GROUP, TILE)] * 3 + [shape_of(8, TILE, dtype=F32)],
        [whole(da.shape), whole(db.shape), of_layer(layer, ATTN)] + [whole(q.shape)] * 3 + [whole(table.shape), whole(mask.shape)],
        da, db, weights, q, k, v, table, mask,
        flops=2 * GROUP * D * ATTN,
    )


def attention_grads_kernel(na_ref, nb_ref, o_ref, da_ref, db_ref, dq_ref, dk_ref, dv_ref, vec_ref, out_ref):
    n = both(na_ref, nb_ref)
    dattn = both(da_ref, db_ref)
    o = o_ref[...]
    parts = (dq_ref[...], dk_ref[...], dv_ref[...])
    for b in range(BLOCKS):
        left = n[:, TILE * b : TILE * (b + 1)]
        for j in range(3):
            half, row = divmod(TILE * j, 2 * TILE)
            out_ref[half, b, row : row + TILE, :] = dot_tn(left, parts[j]).astype(BF16)
    for j in range(BLOCKS):
        part = dot_tn(o, dattn[:, TILE * j : TILE * (j + 1)]).astype(BF16)
        out_ref[1, :, TILE + 32 * j : TILE + 32 * (j + 1), :] = part.reshape(BLOCKS, 32, TILE)
    out_ref[0, :, 2 * TILE :, :] = vec_ref[...]
    out_ref[1, :, 2 * TILE :, :] = jnp.zeros_like(vec_ref)


def attention_grads(na, nb, o, da, db, dq, dk, dv, vec):
    args = (na, nb, o, da, db, dq, dk, dv, vec)
    return call(
        attention_grads_kernel,
        [shape_of(2, BLOCKS, ATTN // 2 + VEC, TILE)],
        [whole(a.shape) for a in args],
        *args,
        flops=2 * GROUP * D * ATTN,
    )[0]


def feed_grads_kernel(na_ref, nb_ref, dg_ref, du_ref, act_ref, ma_ref, mb_ref, vec_ref, out_ref):
    n = both(na_ref, nb_ref)
    gm = both(ma_ref, mb_ref)
    act = act_ref[...]
    for b in range(BLOCKS):
        left = n[:, TILE * b : TILE * (b + 1)]
        for half, ref in enumerate((dg_ref, du_ref)):
            for j in range(3):
                lanes = slice(TILE * j, TILE * (j + 1))
                out_ref[half, b, lanes, :] = dot_tn(left, ref[:, lanes]).astype(BF16)
    for j in range(BLOCKS):
        half, k = divmod(j, 4)
        part = dot_tn(act, gm[:, TILE * j : TILE * (j + 1)]).astype(BF16)
        row = 3 * TILE + PADDED * k
        out_ref[half, :, row : row + PADDED, :] = part.reshape(BLOCKS, PADDED, TILE)
    out_ref[0, :, MLP // 2 :, :] = vec_ref[...]
    out_ref[1, :, MLP // 2 :, :] = jnp.zeros_like(vec_ref)


def feed_grads(na, nb, dg, du, act, ma, mb, vec):
    args = (na, nb, dg, du, act, ma, mb, vec)
    return call(
        feed_grads_kernel,
        [shape_of(2, BLOCKS, MLP // 2 + VEC, TILE)],
        [whole(a.shape) for a in args],
        *args,
        flops=2 * GROUP * D * MLP,
    )[0]


def turned(block, axis, step):
    n = math.prod(lax.axis_size(a) for a in (axis if isinstance(axis, tuple) else (axis,)))
    return lax.ppermute(block, axis, [(i, (i - step) % n) for i in range(n)])


def in_order(block, axis, n):
    ahead = jnp.stack([block] + [turned(block, axis, k) for k in range(1, n)])
    return jnp.roll(ahead, lax.axis_index(axis), axis=0)


def gathered_rows(block):
    own = jnp.concatenate([block] + [turned(block, "x", k) for k in range(1, 4)], axis=0)
    return own, turned(own, "core", 1)


def summed_rows(part_a, part_b):
    other = turned(part_b, "core", 1)

    def piece(k):
        rows = slice(ROWS * k, ROWS * (k + 1))
        return part_a[rows].astype(F32) + other[rows].astype(F32)

    arrived = [turned(piece(k).astype(BF16), "x", -k) for k in (1, 2, 3)]
    total = piece(0)
    for block in arrived:
        total = total + block.astype(F32)
    return total


def swapped(block):
    return lax.ppermute(block, ("y", "core"), [(2 * y + c, 2 * c + y) for y in range(2) for c in range(2)])


def spread(block):
    return lax.all_to_all(block, ("x", "core"), 0, 0, tiled=True)


def to_stored(rows):
    shape = rows.shape[:-1]
    k = len(shape)
    cut = rows.reshape(*shape, 4, 8, 64)
    return jnp.swapaxes(cut, k, k + 1).reshape(*shape, D)


def from_stored(rows):
    shape = rows.shape[:-1]
    k = len(shape)
    cut = rows.reshape(*shape, 8, 4, 64)
    return jnp.swapaxes(cut, k, k + 1).reshape(*shape, D)


def cut_out(weight):
    rows = weight.shape[0]
    return weight.reshape(rows, 4, 8, 64).transpose(2, 0, 1, 3).reshape(8, rows, TILE)


def join_out(blocks):
    rows = blocks.shape[1]
    return blocks.reshape(8, rows, 4, 64).transpose(1, 2, 0, 3).reshape(rows, D)


def value_columns(cut):
    shape = cut.shape[:-1]
    k = len(shape)
    return jnp.swapaxes(cut.reshape(*shape, 4, 2, 32), k, k + 1).reshape(*shape, TILE)


def value_columns_back(cut):
    shape = cut.shape[:-1]
    k = len(shape)
    return jnp.swapaxes(cut.reshape(*shape, 2, 4, 32), k, k + 1).reshape(*shape, TILE)


def pad_pieces(array, axis):
    pads = [(0, 0)] * array.ndim
    pads[axis] = (0, PADDED - PIECE)
    return jnp.pad(array, pads)


def attention_payload(qkv_weight, out_weight):
    cut = qkv_weight.reshape(32, 3, 8, TILE)
    cut = jnp.concatenate([cut[:, :2], value_columns(cut[:, 2:])], axis=1)
    cut = spread(cut.transpose(2, 1, 0, 3))
    cut = cut.transpose(1, 0, 2, 3).reshape(3 * TILE, TILE)
    return cut, cut_out(out_weight)


def feed_payload(gate_up, down_weight):
    cut = gate_up.reshape(32, 2, 8, 4, 2, PIECE).transpose(2, 1, 0, 4, 3, 5)
    cut = pad_pieces(cut, 5).reshape(8, 2, 32, 3, TILE).transpose(0, 1, 3, 2, 4)
    cut = spread(cut.reshape(8, 6, 32, TILE))
    cut = cut.transpose(1, 0, 2, 3).reshape(6 * TILE, TILE)
    return cut, pad_pieces(cut_out(down_weight), 1)


def attention_owned(full):
    cut = full[: 3 * TILE].reshape(3, 8, 32, TILE).transpose(1, 0, 2, 3)
    cut = spread(cut).transpose(2, 1, 0, 3)
    cut = jnp.concatenate([cut[:, :2], value_columns_back(cut[:, 2:])], axis=1)
    out = swapped(full[3 * TILE :]).reshape(8, 32, TILE)
    return cut.reshape(32, 3 * D).astype(F32), join_out(out).astype(F32)


def feed_owned(gate_up, down):
    cut = gate_up.reshape(6, 8, 32, TILE).transpose(1, 0, 2, 3)
    cut = spread(cut).reshape(8, 2, 3, 32, TILE).transpose(0, 1, 3, 2, 4)
    cut = cut.reshape(8, 2, 32, 2, 4, PADDED)[..., :PIECE]
    cut = cut.transpose(2, 1, 0, 4, 3, 5).reshape(32, 2 * FF)
    down = swapped(down).reshape(8, PADDED, TILE)[:, :PIECE]
    return cut.astype(F32), join_out(down).astype(F32)


def geometry(segments):
    groups = segments.reshape(GROUP // 128, 128)
    index = jnp.arange(128, dtype=jnp.int32)
    block = index // 32
    same = (groups[:, :, None] == groups[:, None, :]) & (block[None, :, None] == block[None, None, :])
    before = index[None, :] < index[:, None]
    places = jnp.sum(jnp.where(same & before, 1.0, 0.0), axis=-1).astype(F32).reshape(GROUP)
    inverse = 10000.0 ** (-(jnp.arange(ROT // 2).astype(F32) * 2.0 / ROT))
    theta = places[:, None] * inverse
    cosine, sine = jnp.cos(theta), jnp.sin(theta)
    rest = HEAD_DIM - ROT
    zero = jnp.zeros((GROUP, ROT // 2), F32)
    straight = jnp.concatenate([cosine, cosine, jnp.ones((GROUP, rest), F32)], axis=1)
    first = jnp.concatenate([-sine, zero, jnp.zeros((GROUP, rest), F32)], axis=1)
    second = jnp.concatenate([zero, sine, jnp.zeros((GROUP, rest), F32)], axis=1)
    table = jnp.stack([jnp.concatenate([t, t], axis=1) for t in (straight, first, second)])
    linked = same & (index[None, :] <= index[:, None])
    return table, jnp.where(linked, 1.0, 0.0).astype(F32).reshape(GROUP, 128)


def normalize(values, gain, shift):
    mean = jnp.mean(values, axis=-1, keepdims=True)
    centred = values - mean
    scale = lax.rsqrt(jnp.mean(centred * centred, axis=-1, keepdims=True) + EPSILON)
    unit = centred * scale
    return (unit * gain + shift).astype(BF16), unit, scale


def normalize_back(grad_out, unit, scale, gain):
    grad_unit = grad_out * gain
    return scale * (
        grad_unit
        - jnp.mean(grad_unit, axis=-1, keepdims=True)
        - unit * jnp.mean(grad_unit * unit, axis=-1, keepdims=True)
    )


def vector_rows(*parts):
    cut = jnp.concatenate(parts, axis=2).astype(BF16)
    return jnp.pad(cut, ((0, 0), (0, VEC - 8), (0, TILE - cut.shape[2])))


def by_owner(vector):
    return vector.reshape(8, 8, 32)


def on_device(
    block_input,
    segment_ids,
    cotangent,
    first_gain,
    first_shift,
    qkv_weight,
    qkv_bias,
    out_weight,
    second_gain,
    second_shift,
    gate_up,
    down_weight,
):
    section = lax.axis_index("section")
    shard = 2 * lax.axis_index("x") + lax.axis_index("core")

    qkv_part, out_part = attention_payload(qkv_weight[0], out_weight[0])
    gate_part, down_part = feed_payload(gate_up[0], down_weight[0])
    out_part = swapped(out_part).reshape(TILE, TILE)
    down_part = swapped(down_part).reshape(3 * TILE, TILE)
    attn_weights = lax.all_gather(jnp.concatenate([qkv_part, out_part], axis=0), SPREAD, axis=0, tiled=True)
    attn_weights = attn_weights.reshape(2, BLOCKS, ATTN, TILE)
    feed_weights = lax.all_gather(jnp.concatenate([gate_part, down_part], axis=0), SPREAD, axis=0, tiled=True)
    feed_weights = feed_weights.reshape(2, BLOCKS, MLP, TILE)

    vectors = jnp.concatenate([first_gain[0], first_shift[0], second_gain[0], second_shift[0], qkv_bias[0]])
    vectors = jnp.pad(vectors, (0, 32)).reshape(1, TILE)
    vectors = in_order(vectors, "core", 2)
    vectors = in_order(vectors, "x", 4)
    vectors = in_order(vectors, "z", 4)
    vectors = in_order(vectors, RING, 4)
    vectors = vectors.reshape(2, 64, TILE).astype(F32)
    gains = [vectors[:, :, 32 * k : 32 * (k + 1)].reshape(2, D) for k in range(4)]
    bias = vectors[:, :, 128:224].reshape(2, 2, 4, 4, 2, 96).transpose(0, 3, 1, 2, 4, 5).reshape(2, 3, 8, TILE)
    bias = lax.dynamic_index_in_dim(bias, shard, 2, keepdims=False)
    bias = jnp.concatenate([bias[:, :2], value_columns(bias[:, 2:])], axis=1)
    bias = jnp.pad(bias, ((0, 0), (0, 5), (0, 0)))

    def own_rows(array):
        return lax.dynamic_slice_in_dim(array, 2 * section, 2, 0)

    rows_in = to_stored(own_rows(block_input).reshape(ROWS, D))
    top_grad = to_stored(own_rows(cotangent).reshape(ROWS, D))
    segments = own_rows(segment_ids).reshape(1, ROWS)
    seg_a, seg_b = gathered_rows(segments)
    table, mask = geometry(jnp.concatenate([seg_a, seg_b], axis=0))
    top_a, top_b = gathered_rows(top_grad)

    kept = []
    outputs = []
    layer_in = rows_in
    for layer in range(2):
        inputs = layer_in.astype(F32)
        n1, unit1, scale1 = normalize(inputs, gains[0][layer], gains[1][layer])
        n1a, n1b = gathered_rows(n1)
        part_a, part_b, q, k, v, mixed = attention(layer, n1a, n1b, attn_weights, bias[layer], table, mask)
        hidden = inputs + summed_rows(part_a, part_b)
        n2, unit2, scale2 = normalize(hidden, gains[2][layer], gains[3][layer])
        n2a, n2b = gathered_rows(n2)
        part_a, part_b, g, u, act = feed(layer, n2a, n2b, feed_weights)
        result = (hidden + summed_rows(part_a, part_b)).astype(BF16)
        outputs.append(result)
        layer_in = result
        kept.append((unit1, scale1, n1a, n1b, q, k, v, mixed, unit2, scale2, n2a, n2b, g, u, act))

    grads_in = [None, None]
    attn_sums = [None, None]
    feed_sums = [None, None]
    upstream = top_grad
    ma, mb = top_a, top_b
    for layer in (1, 0):
        unit1, scale1, n1a, n1b, q, k, v, mixed, unit2, scale2, n2a, n2b, g, u, act = kept[layer]
        if layer == 0:
            ma, mb = gathered_rows(upstream)
        ea, eb, dg, du = feed_back(layer, ma, mb, feed_weights, g, u)
        e2 = summed_rows(ea, eb)
        grad_hidden = upstream.astype(F32) + normalize_back(e2, unit2, scale2, gains[2][layer])
        dattn = grad_hidden.astype(BF16)
        da, db = gathered_rows(dattn)
        feed_sums[layer] = feed_grads(
            n2a, n2b, dg, du, act, ma, mb,
            vector_rows(by_owner(jnp.sum(e2 * unit2, axis=0)), by_owner(jnp.sum(e2, axis=0))),
        )
        ea, eb, dq, dk, dv, bias_sum = attention_back(layer, da, db, attn_weights, q, k, v, table, mask)
        e1 = summed_rows(ea, eb)
        grad_rows = grad_hidden + normalize_back(e1, unit1, scale1, gains[0][layer])
        bias_sum = jnp.concatenate([bias_sum[:2], value_columns_back(bias_sum[2:3])], axis=0)
        bias_sum = lax.dynamic_update_slice_in_dim(jnp.zeros((3, 8, TILE), F32), bias_sum[:, None], shard, 1)
        bias_sum = bias_sum.reshape(4, 2, 4, 2, 96).transpose(1, 2, 0, 3, 4).reshape(8, 8, 96)
        attn_sums[layer] = attention_grads(
            n1a, n1b, mixed, da, db, dq, dk, dv,
            vector_rows(by_owner(jnp.sum(e1 * unit1, axis=0)), by_owner(jnp.sum(e1, axis=0)), bias_sum),
        )
        grads_in[layer] = grad_rows
        upstream = grad_rows.astype(BF16)

    def scattered(parts):
        joined = jnp.concatenate(parts, axis=2) if len(parts) > 1 else parts[0]
        joined = joined.reshape(16, -1, TILE)
        return lax.psum_scatter(joined, SPREAD, scatter_dimension=0, tiled=False)

    attn_rows = ATTN // 2 + VEC
    feed_1 = scattered([feed_sums[1]])
    middle = scattered([attn_sums[1], feed_sums[0]])
    attn_1, feed_0 = middle[:attn_rows], middle[attn_rows:]
    attn_0 = scattered([attn_sums[0]])

    def whole_layer(low, high):
        mine = jnp.where(section == 0, low, high)
        other = turned(jnp.where(section == 0, high, low), "section", 1)
        first = jnp.where(section == 0, mine, other)
        second = jnp.where(section == 0, other, mine)
        return first, second

    feed_first, feed_second = whole_layer(feed_0, feed_1)
    attn_first, attn_second = whole_layer(attn_0, attn_1)
    gate_up_grad, down_grad = feed_owned(
        jnp.concatenate([feed_first[: 3 * TILE], feed_second[: 3 * TILE]], axis=0),
        jnp.concatenate([feed_first[3 * TILE : MLP // 2], feed_second[3 * TILE : MLP // 2]], axis=0),
    )
    qkv_grad, out_grad = attention_owned(
        jnp.concatenate([attn_first[: 2 * TILE], attn_second[: 2 * TILE]], axis=0)
    )
    small = jnp.concatenate([attn_first[2 * TILE : 2 * TILE + 8], feed_first[MLP // 2 : MLP // 2 + 8]], axis=1)
    small = jnp.sum(spread(small).astype(F32), axis=0)

    def layer_rows(first, second):
        mine = jnp.where(section == 0, first, second)
        other = turned(jnp.where(section == 0, second, first).astype(BF16), "section", 1).astype(first.dtype)
        rows = jnp.where(section == 0, jnp.concatenate([mine, other]), jnp.concatenate([other, mine]))
        return from_stored(rows).reshape(1, 4, 32, D)

    activations = layer_rows(outputs[0], outputs[1])
    input_grads = layer_rows(grads_in[0], upstream_of(grads_in[1]))
    return (
        activations,
        input_grads,
        small[None, 0:32],
        small[None, 32:64],
        qkv_grad[None],
        small[None, 64:160],
        out_grad[None],
        small[None, TILE : TILE + 32],
        small[None, TILE + 32 : TILE + 64],
        gate_up_grad[None],
        down_grad[None],
    )


def upstream_of(grad_rows):
    return grad_rows.astype(BF16).astype(F32)


def solution(mesh):
    grid = Mesh(mesh.devices.reshape(2, 4, 2, 4, 2), GRID)
    return jax.shard_map(
        on_device,
        mesh=grid,
        in_specs=(
            P(None, DP, None),
            P(None, DP),
            P(None, DP, None),
            P("section", DP),
            P("section", DP),
            P("section", DP, None),
            P("section", DP),
            P("section", DP, None),
            P("section", DP),
            P("section", DP),
            P("section", DP, None),
            P("section", DP, None),
        ),
        out_specs=(
            P("section", None, DP, None),
            P("section", None, DP, None),
            P("section", DP),
            P("section", DP),
            P("section", DP, None),
            P("section", DP),
            P("section", DP, None),
            P("section", DP),
            P("section", DP),
            P("section", DP, None),
            P("section", DP, None),
        ),
        check_vma=False,
    )
```

```python
import functools
import math

import jax
import jax.numpy as jnp
import numpy as np
from jax import lax
from jax.experimental import pallas as pl
from jax.experimental.pallas import tpu as pltpu
from jax.sharding import Mesh
from jax.sharding import PartitionSpec as P

D = 2048
HEAD_DIM = 64
ROT = 16
FF = 5632
EPSILON = 1e-05
NEG_FILL = -1e30
TILE = 256
BLOCKS = D // TILE
ROWS = 64
GROUP = 8 * ROWS
HALF = GROUP // 2
PIECE = 88
PADDED = 96
WIDE = 8 * PADDED
DOWN = 4 * PADDED
VEC = 16
ATTN = 2 * TILE
FEED = 3 * TILE + DOWN
LAYER = ATTN + FEED
SUMS = LAYER + 2 * VEC
VMEM = 40 * 1024 * 1024
F32 = jnp.float32
BF16 = jnp.bfloat16

GRID = ("section", "x", "y", "z", "core")
DP = ("x", "y", "z", "core")
RING = ("section", "y")
SPREAD = ("section", "y", "z")


def dot(a, b):
    return jnp.dot(a, b, preferred_element_type=F32)


def dot_nt(a, b):
    return lax.dot_general(a, b, (((1,), (1,)), ((), ())), preferred_element_type=F32)


def dot_tn(a, b):
    return lax.dot_general(a, b, (((0,), (0,)), ((), ())), preferred_element_type=F32)


def shape_of(*dims, dtype=BF16):
    return jax.ShapeDtypeStruct(dims, dtype)


def in_vmem():
    return pl.BlockSpec(memory_space=pltpu.VMEM)


def in_hbm():
    return pl.BlockSpec(memory_space=pltpu.HBM)


def without(kernel, place):
    def run(*refs):
        kernel(*refs[:place], *refs[place + 1 :])

    return run


def call(kernel, args, outs, *, flops, hbm=0, scratch=(), in_place=False, stay=0, to_hbm=False, after=None):
    stay = len(outs) if stay == 0 else stay
    kept = [pltpu.VMEM(o.shape, o.dtype) for o in outs[stay:]]
    scratch = [*scratch, *kept]
    if kept:
        scratch.append(pltpu.SemaphoreType.DMA((len(kept),)))
    moved = sum(math.prod(o.shape) * o.dtype.itemsize for o in outs)
    moved += sum(math.prod(a.shape) * a.dtype.itemsize for a in args)
    in_specs = [in_hbm() if k < hbm else in_vmem() for k in range(len(args))]
    if after is not None:
        kernel = without(kernel, len(args))
        args = (*args, after)
        in_specs.append(in_hbm())
    return pl.pallas_call(
        kernel,
        in_specs=in_specs,
        out_specs=[in_hbm() if to_hbm or k >= stay else in_vmem() for k in range(len(outs))],
        out_shape=outs,
        scratch_shapes=scratch,
        input_output_aliases={0: 0} if in_place else {},
        compiler_params=pltpu.CompilerParams(vmem_limit_bytes=VMEM),
        cost_estimate=pl.CostEstimate(flops=flops, bytes_accessed=min(moved, 16 * 1024 * 1024), transcendentals=0),
    )(*args)


def rows_of(refs):
    return jnp.concatenate([r[...] for r in refs], axis=0)


class Kept:
    def __init__(self, targets, refs):
        self.targets, self.held, self.sems = targets, refs[:-1], refs[-1]
        self.copies = []

    def send(self, k):
        copy = pltpu.make_async_copy(self.held[k], self.targets[k], self.sems.at[k])
        copy.start()
        self.copies.append(copy)

    def wait(self):
        for copy in self.copies:
            copy.wait()


class Weights:
    def __init__(self, source, held, sems, pieces):
        self.held = held
        self.copies = []
        for k, (half, row, count, to) in enumerate(pieces):
            copy = pltpu.make_async_copy(
                source.at[half, :, row : row + count, :], held.at[:, to : to + count, :], sems.at[k]
            )
            copy.start()
            self.copies.append(copy)

    def wait(self, k):
        self.copies[k].wait()

    def tile(self, row, count=TILE):
        return self.held[:, row : row + count, :].reshape(BLOCKS * count, TILE)

    def block(self, b, row):
        return self.held[b, row : row + TILE, :]


def lane_head(width, of):
    lane = lax.broadcasted_iota(jnp.int32, (128, TILE), 1)
    return (lane // width) % 4 == of


def stacked(array, width):
    zero = jnp.zeros((), array.dtype)
    return jnp.concatenate([jnp.where(lane_head(width, h), array, zero) for h in range(4)], axis=0)


def unstacked(array, width):
    out = jnp.where(lane_head(width, 0), array[:128], 0.0)
    for h in range(1, 4):
        out = jnp.where(lane_head(width, h), array[128 * h : 128 * (h + 1)], out)
    return out


def twisted(u, table_ref, sign):
    def wide(k):
        t = table_ref[k]
        return jnp.concatenate([t, t], axis=1)

    n = u.shape[1]
    half = ROT // 2
    side = pltpu.roll(u, n - half, 1) * wide(1) + pltpu.roll(u, half, 1) * wide(2)
    return u * wide(0) + (side if sign > 0 else -side)


def probabilities(qs, k, mask):
    s = dot_nt(qs, k) * HEAD_DIM**-0.5
    s = jnp.where(jnp.concatenate([mask] * 4, axis=0) > 0, s, NEG_FILL)
    e = jnp.exp(s - jnp.max(s, axis=1, keepdims=True))
    return e / jnp.sum(e, axis=1, keepdims=True)


def put_halves(a_ref, b_ref, j, part):
    part = part.astype(BF16)
    a_ref[:, TILE * j : TILE * (j + 1)] = part[:HALF]
    b_ref[:, TILE * j : TILE * (j + 1)] = part[HALF:]


def attention_kernel(w_ref, *refs):
    n_refs, (bias_ref, table_ref, mask_ref, pa_ref, pb_ref), refs = refs[:8], refs[8:13], refs[13:]
    targets, held, sems, kept = refs[:5], refs[5], refs[6], Kept(refs[:5], refs[7:])
    weights = Weights(w_ref, held, sems, [(t // 2, TILE * (t % 2), TILE, TILE * t) for t in range(4)])
    n_ref, q_ref, k_ref, v_ref, o_ref = kept.held
    n = rows_of(n_refs)
    n_ref[...] = n
    kept.send(0)
    for j, ref in enumerate((q_ref, k_ref, v_ref)):
        weights.wait(j)
        u = dot(n, weights.tile(TILE * j)) + bias_ref[j : j + 1, :]
        ref[...] = (twisted(u, table_ref, 1) if j < 2 else u).astype(BF16)
        kept.send(1 + j)
    for g in range(GROUP // 128):
        rows = slice(128 * g, 128 * g + 128)
        p = probabilities(stacked(q_ref[rows, :], HEAD_DIM), k_ref[rows, :], mask_ref[rows, :])
        o_ref[rows, :] = unstacked(dot(p.astype(BF16), v_ref[rows, :]), 32).astype(BF16)
    kept.send(4)
    o = o_ref[...]
    weights.wait(3)
    for j in range(BLOCKS):
        put_halves(pa_ref, pb_ref, j, dot(o, weights.tile(3 * TILE + 32 * j, 32)))
    kept.wait()


def attention(after, weights, blocks, bias, table, mask):
    return call(
        attention_kernel,
        (weights, *blocks, bias, table, mask),
        [shape_of(HALF, D), shape_of(HALF, D), shape_of(GROUP, D)] + [shape_of(GROUP, TILE)] * 4,
        hbm=1,
        stay=2,
        after=after,
        flops=2 * GROUP * D * 4 * TILE,
        scratch=[pltpu.VMEM((BLOCKS, 4 * TILE, TILE), BF16), pltpu.SemaphoreType.DMA((4,))],
    )


def feed_pieces():
    first = []
    for j in range(3):
        first.append((0, ATTN + TILE * j, TILE, TILE * j))
        first.append((1, ATTN + TILE * j, TILE, TILE * (3 + j)))
    last = [(h, ATTN + 3 * TILE, 4 * PADDED, 6 * TILE + 4 * PADDED * h) for h in range(2)]
    return first, last


FEED_SCRATCH = (BLOCKS, 9 * TILE, TILE)


def feed_kernel(w_ref, *refs):
    n_refs, (pa_ref, pb_ref), refs = refs[:8], refs[8:10], refs[10:]
    held, sems, kept = refs[4], refs[5], Kept(refs[:4], refs[6:])
    first, last = feed_pieces()
    weights = Weights(w_ref, held, sems, first + last)
    n_ref, g_ref, u_ref, act_ref = kept.held
    n = rows_of(n_refs)
    n_ref[...] = n
    kept.send(0)
    for j in range(3):
        lanes = slice(TILE * j, TILE * (j + 1))
        weights.wait(2 * j)
        g = dot(n, weights.tile(TILE * j))
        weights.wait(2 * j + 1)
        u = dot(n, weights.tile(TILE * (3 + j)))
        g_ref[:, lanes] = g
        u_ref[:, lanes] = u
        act_ref[:, lanes] = (g * jax.nn.sigmoid(g) * u).astype(BF16)
    for k in range(1, 4):
        kept.send(k)
    act = act_ref[...]
    for j in range(BLOCKS):
        if j % 4 == 0:
            weights.wait(6 + j // 4)
        put_halves(pa_ref, pb_ref, j, dot(act, weights.tile(6 * TILE + PADDED * j, PADDED)))
    kept.wait()


def feed(after, weights, blocks):
    return call(
        feed_kernel,
        (weights, *blocks),
        [shape_of(HALF, D), shape_of(HALF, D), shape_of(GROUP, D)]
        + [shape_of(GROUP, WIDE, dtype=F32)] * 2
        + [shape_of(GROUP, WIDE)],
        hbm=1,
        stay=2,
        after=after,
        flops=2 * GROUP * D * 9 * TILE,
        scratch=[pltpu.VMEM(FEED_SCRATCH, BF16), pltpu.SemaphoreType.DMA((8,))],
    )


def feed_back_kernel(w_ref, *refs):
    m_refs, (g_ref, u_ref, ea_ref, eb_ref), refs = refs[:8], refs[8:12], refs[12:]
    held, sems, kept = refs[3], refs[4], Kept(refs[:3], refs[5:])
    first, last = feed_pieces()
    weights = Weights(w_ref, held, sems, last + first)
    m_ref, dg_ref, du_ref = kept.held
    gm = rows_of(m_refs)
    m_ref[...] = gm
    kept.send(0)
    da = jnp.zeros((GROUP, WIDE), F32)
    for j in range(BLOCKS):
        if j % 4 == 0:
            weights.wait(j // 4)
        da += dot_nt(gm[:, TILE * j : TILE * (j + 1)], weights.tile(6 * TILE + PADDED * j, PADDED))
    g = g_ref[...]
    u = u_ref[...]
    sigma = jax.nn.sigmoid(g)
    dg_ref[...] = (da * u * sigma * (1.0 + g * (1.0 - sigma))).astype(BF16)
    du_ref[...] = (da * g * sigma).astype(BF16)
    kept.send(1)
    kept.send(2)
    dg = dg_ref[...]
    du = du_ref[...]
    for k in range(6):
        weights.wait(2 + k)
    for b in range(BLOCKS):
        e = jnp.zeros((GROUP, TILE), F32)
        for j in range(3):
            lanes = slice(TILE * j, TILE * (j + 1))
            e += dot_nt(dg[:, lanes], weights.block(b, TILE * j))
            e += dot_nt(du[:, lanes], weights.block(b, TILE * (3 + j)))
        put_halves(ea_ref, eb_ref, b, e)
    kept.wait()


def feed_back(after, weights, blocks, g, u):
    return call(
        feed_back_kernel,
        (weights, *blocks, g, u),
        [shape_of(HALF, D), shape_of(HALF, D), shape_of(GROUP, D)] + [shape_of(GROUP, WIDE)] * 2,
        hbm=1,
        stay=2,
        after=after,
        flops=2 * GROUP * D * 9 * TILE,
        scratch=[pltpu.VMEM(FEED_SCRATCH, BF16), pltpu.SemaphoreType.DMA((8,))],
    )


def attention_back_kernel(w_ref, *refs):
    d_refs = refs[:8]
    q_ref, k_ref, v_ref, table_ref, mask_ref, ea_ref, eb_ref, sum_ref, *refs = refs[8:]
    held, sems, kept = refs[4], refs[5], Kept(refs[:4], refs[6:])
    d_ref, dq_ref, dk_ref, dv_ref = kept.held
    order = (3, 0, 1, 2)
    weights = Weights(w_ref, held, sems, [(t // 2, TILE * (t % 2), TILE, TILE * t) for t in order])
    dattn = rows_of(d_refs)
    d_ref[...] = dattn
    kept.send(0)
    weights.wait(0)
    do = jnp.zeros((GROUP, TILE), F32)
    for j in range(BLOCKS):
        do += dot_nt(dattn[:, TILE * j : TILE * (j + 1)], weights.tile(3 * TILE + 32 * j, 32))
    do = do.astype(BF16)
    dqs, dks = [], []
    for g in range(GROUP // 128):
        rows = slice(128 * g, 128 * g + 128)
        qs = stacked(q_ref[rows, :], HEAD_DIM)
        k = k_ref[rows, :]
        p = probabilities(qs, k, mask_ref[rows, :])
        dos = stacked(do[rows], 32)
        dp = dot_nt(dos, v_ref[rows, :])
        ds = (p * (dp - jnp.sum(p * dp, axis=1, keepdims=True))).astype(BF16)
        dv_ref[rows, :] = dot_tn(p.astype(BF16), dos).astype(BF16)
        dqs.append(unstacked(dot(ds, k), HEAD_DIM))
        dks.append(dot_tn(ds, qs))
    factor = HEAD_DIM**-0.5
    dq_ref[...] = twisted(jnp.concatenate(dqs, axis=0) * factor, table_ref, -1).astype(BF16)
    dk_ref[...] = twisted(jnp.concatenate(dks, axis=0) * factor, table_ref, -1).astype(BF16)
    for k in range(1, 4):
        kept.send(k)
    parts = (dq_ref[...], dk_ref[...], dv_ref[...])
    sums = [jnp.sum(part.astype(F32), axis=0, keepdims=True) for part in parts]
    sum_ref[...] = jnp.concatenate(sums + [jnp.zeros((5, TILE), F32)], axis=0)
    for j in range(3):
        weights.wait(1 + j)
    for b in range(BLOCKS):
        e = jnp.zeros((GROUP, TILE), F32)
        for j in range(3):
            e += dot_nt(parts[j], weights.block(b, TILE * j))
        put_halves(ea_ref, eb_ref, b, e)
    kept.wait()


def attention_back(after, weights, blocks, q, k, v, table, mask):
    return call(
        attention_back_kernel,
        (weights, *blocks, q, k, v, table, mask),
        [shape_of(HALF, D), shape_of(HALF, D), shape_of(8, TILE, dtype=F32), shape_of(GROUP, D)]
        + [shape_of(GROUP, TILE)] * 3,
        hbm=1,
        stay=3,
        after=after,
        flops=2 * GROUP * D * 4 * TILE,
        scratch=[pltpu.VMEM((BLOCKS, 4 * TILE, TILE), BF16), pltpu.SemaphoreType.DMA((4,))],
    )


def send_out(copies, source, target, sem):
    copy = pltpu.make_async_copy(source, target, sem)
    copy.start()
    copies.append(copy)


def feed_grads_kernel(row, *refs):
    n, dg, du, act, gm = [ref[...] for ref in refs[:5]]
    vec_ref, out_ref, held, sems = refs[5:]
    copies = []
    for b in range(BLOCKS):
        left = n[:, TILE * b : TILE * (b + 1)]
        for half, right in enumerate((dg, du)):
            for j in range(3):
                lanes = slice(TILE * j, TILE * (j + 1))
                held[half, b, lanes, :] = dot_tn(left, right[:, lanes]).astype(BF16)
    for j in range(BLOCKS):
        half, k = divmod(j, 4)
        part = dot_tn(act, gm[:, TILE * j : TILE * (j + 1)]).astype(BF16)
        at = 3 * TILE + PADDED * k
        held[half, :, at : at + PADDED, :] = part.reshape(BLOCKS, PADDED, TILE)
    send_out(copies, held, out_ref.at[:, :, row : row + FEED, :], sems.at[0])
    send_out(copies, vec_ref, out_ref.at[:, :, row + FEED : row + FEED + VEC, :], sems.at[1])
    for copy in copies:
        copy.wait()


def feed_grads(after, n, dg, du, act, gm, vec):
    return call(
        functools.partial(feed_grads_kernel, 0),
        (n, dg, du, act, gm, vec),
        [shape_of(2, BLOCKS, SUMS, TILE)],
        after=after,
        flops=2 * GROUP * D * 9 * TILE,
        scratch=[pltpu.VMEM((2, BLOCKS, FEED, TILE), BF16), pltpu.SemaphoreType.DMA((2,))],
        to_hbm=True,
    )[0]


def attention_grads_kernel(row, *refs):
    n, dattn, o, dq, dk, dv = [ref[...] for ref in refs[:6]]
    vec_ref, out_ref, held, sems = refs[6:]
    copies = []
    for b in range(BLOCKS):
        left = n[:, TILE * b : TILE * (b + 1)]
        for j, right in enumerate((dq, dk, dv)):
            half, at = divmod(TILE * j, ATTN)
            held[half, b, at : at + TILE, :] = dot_tn(left, right).astype(BF16)
    for j in range(BLOCKS):
        part = dot_tn(o, dattn[:, TILE * j : TILE * (j + 1)]).astype(BF16)
        held[1, :, TILE + 32 * j : TILE + 32 * (j + 1), :] = part.reshape(BLOCKS, 32, TILE)
    send_out(copies, held, out_ref.at[:, :, row : row + ATTN, :], sems.at[0])
    send_out(copies, vec_ref, out_ref.at[:, :, row + ATTN : row + ATTN + VEC, :], sems.at[1])
    for copy in copies:
        copy.wait()


def attention_grads(after, sums, n, dattn, o, dq, dk, dv, vec):
    return call(
        without(functools.partial(attention_grads_kernel, FEED + VEC), 0),
        (sums, n, dattn, o, dq, dk, dv, vec),
        [shape_of(2, BLOCKS, SUMS, TILE)],
        hbm=1,
        in_place=True,
        after=after,
        flops=2 * GROUP * D * 4 * TILE,
        scratch=[pltpu.VMEM((2, BLOCKS, ATTN, TILE), BF16), pltpu.SemaphoreType.DMA((2,))],
        to_hbm=True,
    )[0]


def add_kernel(a_ref, b_ref, first_ref, *refs):
    for k, ref in enumerate((first_ref, *refs)):
        rows = slice(ROWS * k, ROWS * (k + 1))
        ref[...] = (a_ref[rows, :].astype(F32) + b_ref[rows, :].astype(F32)).astype(ref.dtype)


def added(after, a, b):
    return call(
        add_kernel,
        (a, b),
        [shape_of(ROWS, D, dtype=F32)] + [shape_of(ROWS, D)] * 3,
        flops=HALF * D,
        after=after,
    )


def total_of(refs):
    total = refs[0][...]
    for ref in refs[1:]:
        total = total + ref[...].astype(F32)
    return total


def unit_of(values):
    mean = jnp.mean(values, axis=-1, keepdims=True)
    centred = values - mean
    scale = lax.rsqrt(jnp.mean(centred * centred, axis=-1, keepdims=True) + EPSILON)
    return centred * scale, scale


def norm_kernel(base_ref, *refs):
    parts, (gain_ref, out_ref, n_ref) = refs[:4], refs[4:]
    out = (base_ref[...].astype(F32) + total_of(parts)).astype(out_ref.dtype)
    out_ref[...] = out
    unit, _ = unit_of(out.astype(F32))
    n_ref[...] = (unit * gain_ref[0:1, :] + gain_ref[1:2, :]).astype(BF16)


def normed(after, base, parts, gain, dtype):
    return call(
        norm_kernel,
        (base, *parts, gain),
        [shape_of(ROWS, D, dtype=dtype), shape_of(ROWS, D)],
        flops=16 * ROWS * D,
        after=after,
    )


def norm_back_kernel(up_ref, *refs):
    parts, (values_ref, gain_ref, grad_ref, low_ref, sum_ref) = refs[:4], refs[4:]
    e = total_of(parts)
    unit, scale = unit_of(values_ref[...].astype(F32))
    q = e * gain_ref[0:1, :]
    back = scale * (q - jnp.mean(q, axis=-1, keepdims=True) - unit * jnp.mean(q * unit, axis=-1, keepdims=True))
    grad = up_ref[...].astype(F32) + back
    grad_ref[...] = grad
    low_ref[...] = grad.astype(BF16)
    sums = [jnp.sum(e * unit, axis=0, keepdims=True), jnp.sum(e, axis=0, keepdims=True)]
    sum_ref[...] = jnp.concatenate(sums + [jnp.zeros((6, D), F32)], axis=0)


def normed_back(after, up, parts, values, gain):
    return call(
        norm_back_kernel,
        (up, *parts, values, gain),
        [shape_of(ROWS, D, dtype=F32), shape_of(ROWS, D), shape_of(8, D, dtype=F32)],
        flops=32 * ROWS * D,
        after=after,
    )


def feed_both_kernel(w_ref, *refs):
    n_refs, m_refs = refs[:8], refs[8:16]
    pa_ref, pb_ref, ea_ref, eb_ref, *refs = refs[16:]
    held, sems, kept = refs[5], refs[6], Kept(refs[:5], refs[7:])
    n_ref, m_ref, act_ref, dg_ref, du_ref = kept.held
    first, last = feed_pieces()
    weights = Weights(w_ref, held, sems, last + first)
    n = rows_of(n_refs)
    gm = rows_of(m_refs)
    n_ref[...] = n
    m_ref[...] = gm
    kept.send(0)
    kept.send(1)
    weights.wait(0)
    weights.wait(1)
    for j in range(3):
        lanes = slice(TILE * j, TILE * (j + 1))
        weights.wait(2 + 2 * j)
        g = dot(n, weights.tile(TILE * j))
        weights.wait(3 + 2 * j)
        u = dot(n, weights.tile(TILE * (3 + j)))
        da = jnp.zeros((GROUP, TILE), F32)
        for b in range(BLOCKS):
            w = weights.tile(6 * TILE + PADDED * b, PADDED)[lanes]
            da += dot_nt(gm[:, TILE * b : TILE * (b + 1)], w)
        sigma = jax.nn.sigmoid(g)
        act_ref[:, lanes] = (g * sigma * u).astype(BF16)
        dg_ref[:, lanes] = (da * u * sigma * (1.0 + g * (1.0 - sigma))).astype(BF16)
        du_ref[:, lanes] = (da * g * sigma).astype(BF16)
    for k in range(2, 5):
        kept.send(k)
    act = act_ref[...]
    dg = dg_ref[...]
    du = du_ref[...]
    for b in range(BLOCKS):
        e = jnp.zeros((GROUP, TILE), F32)
        for j in range(3):
            lanes = slice(TILE * j, TILE * (j + 1))
            e += dot_nt(dg[:, lanes], weights.block(b, TILE * j))
            e += dot_nt(du[:, lanes], weights.block(b, TILE * (3 + j)))
        put_halves(ea_ref, eb_ref, b, e)
        put_halves(pa_ref, pb_ref, b, dot(act, weights.tile(6 * TILE + PADDED * b, PADDED)))
    kept.wait()


def feed_both(after, weights, blocks, top):
    return call(
        feed_both_kernel,
        (weights, *blocks, *top),
        [shape_of(HALF, D)] * 4 + [shape_of(GROUP, D)] * 2 + [shape_of(GROUP, WIDE)] * 3,
        hbm=1,
        stay=4,
        after=after,
        flops=4 * GROUP * D * 9 * TILE,
        scratch=[pltpu.VMEM(FEED_SCRATCH, BF16), pltpu.SemaphoreType.DMA((8,))],
    )


def pieces_in_order():
    place = np.zeros((WIDE, 8 * PIECE), np.float32)
    for z in range(4):
        for c in range(2):
            for k in range(PIECE):
                place[(4 * c + z) * PADDED + k, (2 * z + c) * PIECE + k] = 1.0
    return jnp.asarray(place, BF16)


def values_in_order():
    place = np.zeros((TILE, TILE), np.float32)
    for head in range(4):
        for half in range(2):
            for k in range(32):
                place[(half * 4 + head) * 32 + k, (head * 2 + half) * 32 + k] = 1.0
    return jnp.asarray(place, BF16)


def columns_of(ref, b):
    return jnp.concatenate([ref[:, 64 * (8 * x + b) : 64 * (8 * x + b + 1)] for x in range(4)], axis=1)


def pack_kernel(qkv_ref, gate_ref, out_ref, down_ref, places_ref, values_ref, cut_ref, low_ref, high_ref):
    wide = 8 * PIECE
    rows = jnp.concatenate([gate_ref[:, wide * k : wide * (k + 1)] for k in range(16)], axis=0)
    placed = dot_nt(rows, places_ref[...]).astype(BF16)
    values = jnp.concatenate([qkv_ref[:, 2 * D + TILE * t : 2 * D + TILE * (t + 1)] for t in range(8)], axis=0)
    values = dot_nt(values, values_ref[...]).astype(BF16)
    for t in range(8):
        cut_ref[0, t, 0] = qkv_ref[:, TILE * t : TILE * (t + 1)]
        cut_ref[0, t, 1] = qkv_ref[:, D + TILE * t : D + TILE * (t + 1)]
        cut_ref[1, t, 0] = values[32 * t : 32 * (t + 1)]
        cut_ref[1, t, 4] = jnp.zeros((32, TILE), BF16)
        for half in range(2):
            row = 32 * (8 * half + t)
            for j in range(3):
                cut_ref[half, t, 2 - half + j] = placed[row : row + 32, TILE * j : TILE * (j + 1)]
    pad = jnp.zeros((PADDED - PIECE, TILE), BF16)
    for b in range(BLOCKS):
        high_ref[32 * b : 32 * (b + 1), :] = columns_of(out_ref, b)
        down = jnp.concatenate([columns_of(down_ref, b), pad], axis=0)
        row = PADDED * (b % 4)
        if b < 4:
            low_ref[row : row + PADDED, :] = down
        else:
            high_ref[TILE + row : TILE + row + PADDED, :] = down
    low_ref[DOWN:, :] = jnp.zeros((TILE, TILE), BF16)


def packed(qkv_weight, gate_up, out_weight, down_weight):
    return call(
        pack_kernel,
        (qkv_weight, gate_up, out_weight, down_weight, pieces_in_order(), values_in_order()),
        [shape_of(2, 8, 5, 32, TILE), shape_of(DOWN + TILE, TILE), shape_of(DOWN + TILE, TILE)],
        flops=2 * 512 * WIDE * 8 * PIECE,
    )


def put_columns(ref, blocks):
    for x in range(4):
        lanes = slice(64 * x, 64 * (x + 1))
        for k in range(4):
            pair = jnp.concatenate([blocks[2 * k][:, lanes], blocks[2 * k + 1][:, lanes]], axis=1)
            ref[:, 128 * (4 * x + k) : 128 * (4 * x + k + 1)] = pair.astype(F32)


def unpack_kernel(cut_ref, first_ref, second_ref, places_ref, values_ref, qkv_ref, gate_ref, out_ref, down_ref, vec_ref):
    wide = 8 * PIECE
    vec = jnp.zeros((8, TILE), F32)
    for t in range(8):
        qkv_ref[:, TILE * t : TILE * (t + 1)] = cut_ref[0, t, 0].astype(F32)
        qkv_ref[:, D + TILE * t : D + TILE * (t + 1)] = cut_ref[0, t, 1].astype(F32)
        qkv_ref[:, 2 * D + TILE * t : 2 * D + TILE * (t + 1)] = dot(cut_ref[1, t, 0], values_ref[...])
        vec += cut_ref[1, t, 4].astype(F32)[:8]
    vec_ref[...] = vec
    rows = [
        jnp.concatenate([cut_ref[half, t, 2 - half + j] for j in range(3)], axis=1) for half in range(2) for t in range(8)
    ]
    placed = dot(jnp.concatenate(rows, axis=0), places_ref[...])
    for k in range(16):
        gate_ref[:, wide * k : wide * (k + 1)] = placed[32 * k : 32 * (k + 1)]
    put_columns(out_ref, [second_ref[32 * b : 32 * (b + 1), :] for b in range(BLOCKS)])
    down = []
    for b in range(BLOCKS):
        row = PADDED * (b % 4)
        part = first_ref[row : row + PADDED, :] if b < 4 else second_ref[TILE + row : TILE + row + PADDED, :]
        down.append(part.astype(F32)[:PIECE])
    put_columns(down_ref, down)


def unpacked(cut, first, second):
    return call(
        unpack_kernel,
        (cut, first, second, pieces_in_order(), values_in_order()),
        [
            shape_of(32, 3 * D, dtype=F32),
            shape_of(32, 2 * FF, dtype=F32),
            shape_of(32, D, dtype=F32),
            shape_of(PIECE, D, dtype=F32),
            shape_of(8, TILE, dtype=F32),
        ],
        flops=2 * 512 * WIDE * 8 * PIECE,
    )


def turned(block, axis, step):
    n = math.prod(lax.axis_size(a) for a in (axis if isinstance(axis, tuple) else (axis,)))
    return lax.ppermute(block, axis, [(i, (i - step) % n) for i in range(n)])


def in_order(block, axis, n):
    ahead = jnp.stack([block] + [turned(block, axis, k) for k in range(1, n)])
    return jnp.roll(ahead, lax.axis_index(axis), axis=0)


def gathered_rows(block):
    own = [block] + [turned(block, "x", k) for k in range(1, 4)]
    return own + [turned(part, "core", 1) for part in own]


def summed_parts(after, part_a, part_b):
    first, *rest = added(after, part_a, turned(part_b, "core", 1))
    return [first] + [turned(block, "x", -k) for k, block in enumerate(rest, 1)]


def swapped(block, step):
    pairs = []
    for k in range(2):
        for y in range(2):
            for c in range(2):
                pairs.append((4 * k + 2 * y + c, 4 * ((k + step) % 2) + 2 * c + y))
    return lax.ppermute(block, ("section", "y", "core"), pairs)


def spread(block):
    return lax.all_to_all(block, ("section", "x", "core"), 0, 0, tiled=True)


def scattered(array):
    array = array.reshape(16, -1, TILE)
    return lax.optimization_barrier(lax.psum_scatter(array, SPREAD, scatter_dimension=0, tiled=False))


def to_stored(rows):
    shape = rows.shape[:-1]
    k = len(shape)
    cut = rows.reshape(*shape, 4, 8, 64)
    return jnp.swapaxes(cut, k, k + 1).reshape(*shape, D)


def from_stored(rows):
    shape = rows.shape[:-1]
    k = len(shape)
    cut = rows.reshape(*shape, 8, 4, 64)
    return jnp.swapaxes(cut, k, k + 1).reshape(*shape, D)


def value_columns(cut):
    shape = cut.shape[:-1]
    k = len(shape)
    return jnp.swapaxes(cut.reshape(*shape, 4, 2, 32), k, k + 1).reshape(*shape, TILE)


def value_columns_back(cut):
    shape = cut.shape[:-1]
    k = len(shape)
    return jnp.swapaxes(cut.reshape(*shape, 2, 4, 32), k, k + 1).reshape(*shape, TILE)


def both_layers(qkv_weight, out_weight, gate_up, down_weight):
    section = lax.axis_index("section")
    cut, low, high = packed(qkv_weight, gate_up, out_weight, down_weight)
    cut = spread(cut.reshape(16, 5, 32, TILE))
    cut = cut.reshape(2, 8, 5, 32, TILE).transpose(0, 2, 1, 3, 4).reshape(2, 5 * TILE, TILE)
    kept = swapped(jnp.where(section == 0, low, high), 0)
    sent = swapped(jnp.where(section == 0, high, low), 1)
    parts = []
    for layer in range(2):
        rows = jnp.where(section == layer, kept, sent)
        low = jnp.concatenate([cut[layer], rows[:DOWN]], axis=0)
        high = jnp.concatenate([cut[layer, :TILE], rows[:TILE], cut[layer, TILE : 4 * TILE], rows[TILE:]], axis=0)
        parts.append(jnp.where(section == 0, low, high))
    return parts


def owned(attn, feed, vecs):
    section = lax.axis_index("section")
    tiles = []
    for layer in range(2):
        low = jnp.concatenate([attn[layer], feed[layer][: 3 * TILE]], axis=0).reshape(5, 8, 32, TILE)
        vec = jnp.pad(jnp.stack(vecs[layer], axis=1), ((0, 0), (0, 30), (0, 0))).reshape(1, 8, 32, TILE)
        high = jnp.concatenate([attn[layer][:TILE], feed[layer][: 3 * TILE]], axis=0).reshape(4, 8, 32, TILE)
        tiles.append(jnp.where(section == 0, low, jnp.concatenate([high, vec], axis=0)))
    cut = spread(jnp.stack(tiles).transpose(0, 2, 1, 3, 4).reshape(16, 5, 32, TILE)).reshape(2, 8, 5, 32, TILE)
    low = [jnp.pad(feed[layer][3 * TILE :], ((0, TILE), (0, 0))) for layer in range(2)]
    high = [jnp.concatenate([attn[layer][TILE:], feed[layer][3 * TILE :]], axis=0) for layer in range(2)]
    kept = swapped(jnp.where(section == 0, low[0], high[1]), 0)
    sent = swapped(jnp.where(section == 0, low[1], high[0]), 1)
    first = jnp.where(section == 0, kept, sent)
    second = jnp.where(section == 0, sent, kept)
    return unpacked(cut, first, second)


def geometry(segments):
    groups = segments.reshape(GROUP // 128, 128)
    index = jnp.arange(128, dtype=jnp.int32)
    block = index // 32
    same = (groups[:, :, None] == groups[:, None, :]) & (block[None, :, None] == block[None, None, :])
    before = index[None, :] < index[:, None]
    places = jnp.sum(jnp.where(same & before, 1.0, 0.0), axis=-1).astype(F32).reshape(GROUP)
    inverse = 10000.0 ** (-(jnp.arange(ROT // 2).astype(F32) * 2.0 / ROT))
    theta = places[:, None] * inverse
    cosine, sine = jnp.cos(theta), jnp.sin(theta)
    rest = HEAD_DIM - ROT
    zero = jnp.zeros((GROUP, ROT // 2), F32)
    straight = jnp.concatenate([cosine, cosine, jnp.ones((GROUP, rest), F32)], axis=1)
    first = jnp.concatenate([-sine, zero, jnp.zeros((GROUP, rest), F32)], axis=1)
    second = jnp.concatenate([zero, sine, jnp.zeros((GROUP, rest), F32)], axis=1)
    table = jnp.stack([jnp.concatenate([t, t], axis=1) for t in (straight, first, second)])
    linked = same & (index[None, :] <= index[:, None])
    return table, jnp.where(linked, 1.0, 0.0).astype(F32).reshape(GROUP, 128)


def vector_rows(*parts):
    cut = jnp.concatenate(parts, axis=2).astype(BF16)
    cut = jnp.pad(cut, ((0, 0), (0, VEC - 8), (0, TILE - cut.shape[2])))
    return jnp.stack([jnp.zeros_like(cut), cut])


def by_owner(vector):
    return vector.reshape(8, 8, 32)


def on_device(
    block_input,
    segment_ids,
    cotangent,
    first_gain,
    first_shift,
    qkv_weight,
    qkv_bias,
    out_weight,
    second_gain,
    second_shift,
    gate_up,
    down_weight,
):
    section = lax.axis_index("section")
    shard = 2 * lax.axis_index("x") + lax.axis_index("core")

    weights = []
    for part in both_layers(qkv_weight[0], out_weight[0], gate_up[0], down_weight[0]):
        full = lax.all_gather(part, SPREAD, axis=0, tiled=True)
        weights.append(full.reshape(2, BLOCKS, LAYER, TILE))

    vectors = jnp.concatenate([first_gain[0], first_shift[0], second_gain[0], second_shift[0], qkv_bias[0]])
    vectors = jnp.pad(vectors, (0, 32)).reshape(1, TILE)
    vectors = in_order(vectors, "core", 2)
    vectors = in_order(vectors, "x", 4)
    vectors = in_order(vectors, "z", 4)
    vectors = in_order(vectors, RING, 4)
    vectors = vectors.reshape(2, 64, TILE).astype(F32)
    gains = [vectors[:, :, 32 * k : 32 * (k + 1)].reshape(2, D) for k in range(4)]
    bias = vectors[:, :, 128:224].reshape(2, 2, 4, 4, 2, 96).transpose(0, 3, 1, 2, 4, 5).reshape(2, 3, 8, TILE)
    bias = lax.dynamic_index_in_dim(bias, shard, 2, keepdims=False)
    bias = jnp.concatenate([bias[:, :2], value_columns(bias[:, 2:])], axis=1)
    bias = jnp.pad(bias, ((0, 0), (0, 5), (0, 0)))

    def own_rows(array):
        return lax.dynamic_slice_in_dim(array, 2 * section, 2, 0)

    rows_in = to_stored(own_rows(block_input).reshape(ROWS, D))
    top_grad = to_stored(own_rows(cotangent).reshape(ROWS, D))
    segments = gathered_rows(own_rows(segment_ids).reshape(1, ROWS))
    tables = geometry(jnp.concatenate(segments, axis=0))
    top = gathered_rows(top_grad)
    first_gains = [jnp.stack([gains[0][layer], gains[1][layer]]) for layer in range(2)]
    second_gains = [jnp.stack([gains[2][layer], gains[3][layer]]) for layer in range(2)]

    outputs = [None, None]
    kept = [{}, {}]
    base = rows_in
    unit, _ = unit_of(base.astype(F32))
    n = (unit * first_gains[0][0:1] + first_gains[0][1:2]).astype(BF16)
    for layer in range(2):
        have = kept[layer]
        part_a, part_b, have["n1"], have["q"], have["k"], have["v"], have["mixed"] = attention(
            None, weights[layer], gathered_rows(n), bias[layer], *tables
        )
        have["values1"] = base
        hidden, n = normed(None, base, summed_parts(None, part_a, part_b), second_gains[layer], F32)
        have["values2"] = hidden
        if layer == 0:
            part_a, part_b, have["n2"], have["g"], have["u"], have["act"] = feed(None, weights[0], gathered_rows(n))
            base, n = normed(None, hidden, summed_parts(None, part_a, part_b), first_gains[1], BF16)
            outputs[0] = base
    part_a, part_b, ea, eb, have["n2"], have["gm"], have["act"], have["dg"], have["du"] = feed_both(
        None, weights[1], gathered_rows(n), top
    )

    def feed_sums(have):
        sums = have["sums2"]
        vec = vector_rows(by_owner(sums[0]), by_owner(sums[1]))
        return feed_grads(None, have["n2"], have["dg"], have["du"], have["act"], have["gm"], vec)

    def attention_sums(have, buffer):
        sums = have["sums1"]
        bias_sum = have["bias_sum"]
        bias_sum = jnp.concatenate([bias_sum[:2], value_columns_back(bias_sum[2:3])], axis=0)
        bias_sum = lax.dynamic_update_slice_in_dim(jnp.zeros((3, 8, TILE), F32), bias_sum[:, None], shard, 1)
        bias_sum = bias_sum.reshape(4, 2, 4, 2, 96).transpose(1, 2, 0, 3, 4).reshape(8, 8, 96)
        vec = vector_rows(by_owner(sums[0]), by_owner(sums[1]), bias_sum)
        names = ("n1", "dattn", "mixed", "dq", "dk", "dv")
        return attention_grads(None, buffer, *(have[name] for name in names), vec)

    grads_in = [None, None]
    up = top_grad
    sums_1 = None
    for layer in (1, 0):
        have = kept[layer]
        if layer == 0:
            ea, eb, have["gm"], have["dg"], have["du"] = feed_back(
                sums_1, weights[0], gathered_rows(up), have["g"], have["u"]
            )
        grad, low, have["sums2"] = normed_back(None, up, summed_parts(None, ea, eb), have["values2"], second_gains[layer])
        buffer = feed_sums(have)
        ea, eb, have["bias_sum"], have["dattn"], have["dq"], have["dk"], have["dv"] = attention_back(
            buffer, weights[layer], gathered_rows(low), have["q"], have["k"], have["v"], *tables
        )
        parts = summed_parts(None, ea, eb)
        grads_in[layer], up, have["sums1"] = normed_back(None, grad, parts, have["values1"], first_gains[layer])
        if layer == 1:
            sums_1 = attention_sums(have, buffer)
    sums_0 = attention_sums(kept[0], buffer)
    first, *rest = summed_parts(sums_0, part_a, part_b)
    total = kept[1]["values2"] + first
    for block in rest:
        total = total + block.astype(F32)
    outputs[1] = total.astype(BF16)

    sum_1 = scattered(sums_1)
    sum_0 = scattered(sums_0)
    feed_0, attn_0 = sum_0[: FEED + VEC], sum_0[FEED + VEC :]
    feed_1, attn_1 = sum_1[: FEED + VEC], sum_1[FEED + VEC :]
    attn = [attn_0[:ATTN], attn_1[:ATTN]]
    feeds = [feed_0[:FEED], feed_1[:FEED]]
    vecs = [(attn_0[ATTN : ATTN + 8], feed_0[FEED : FEED + 8]), (attn_1[ATTN : ATTN + 8], feed_1[FEED : FEED + 8])]
    qkv_grad, gate_up_grad, out_grad, down_grad, small = owned(attn, feeds, vecs)

    def layer_rows(first, second):
        mine = jnp.where(section == 0, first, second)
        other = turned(jnp.where(section == 0, second, first).astype(BF16), "section", 1).astype(first.dtype)
        rows = jnp.where(section == 0, jnp.concatenate([mine, other]), jnp.concatenate([other, mine]))
        return from_stored(rows).reshape(1, 4, 32, D)

    activations = layer_rows(outputs[0], outputs[1])
    input_grads = layer_rows(grads_in[0], upstream_of(grads_in[1]))
    return (
        activations,
        input_grads,
        small[0][None, 0:32],
        small[0][None, 32:64],
        qkv_grad[None],
        small[0][None, 64:160],
        out_grad[None],
        small[1][None, 0:32],
        small[1][None, 32:64],
        gate_up_grad[None],
        down_grad[None],
    )


def upstream_of(grad_rows):
    return grad_rows.astype(BF16).astype(F32)


def solution(mesh):
    grid = Mesh(mesh.devices.reshape(2, 4, 2, 4, 2), GRID)
    return jax.shard_map(
        on_device,
        mesh=grid,
        in_specs=(
            P(None, DP, None),
            P(None, DP),
            P(None, DP, None),
            P("section", DP),
            P("section", DP),
            P("section", DP, None),
            P("section", DP),
            P("section", DP, None),
            P("section", DP),
            P("section", DP),
            P("section", DP, None),
            P("section", DP, None),
        ),
        out_specs=(
            P("section", None, DP, None),
            P("section", None, DP, None),
            P("section", DP),
            P("section", DP),
            P("section", DP, None),
            P("section", DP),
            P("section", DP, None),
            P("section", DP),
            P("section", DP),
            P("section", DP, None),
            P("section", DP, None),
        ),
        check_vma=False,
    )
```

```python
import functools
import math

import jax
import jax.numpy as jnp
import numpy as np
from jax import lax
from jax.experimental import pallas as pl
from jax.experimental.pallas import tpu as pltpu
from jax.sharding import Mesh
from jax.sharding import PartitionSpec as P

D = 2048
HEAD_DIM = 64
ROT = 16
FF = 5632
EPSILON = 1e-05
NEG_FILL = -1e30
TILE = 256
BLOCKS = D // TILE
ROWS = 64
GROUP = 8 * ROWS
HALF = GROUP // 2
PIECE = 88
PADDED = 96
WIDE = 8 * PADDED
DOWN = 4 * PADDED
VEC = 16
ATTN = 2 * TILE
FEED = 3 * TILE + DOWN
LAYER = ATTN + FEED
SUMS = LAYER + 2 * VEC
VMEM = 40 * 1024 * 1024
F32 = jnp.float32
BF16 = jnp.bfloat16

GRID = ("section", "x", "y", "z", "core")
DP = ("x", "y", "z", "core")
RING = ("section", "y")
SPREAD = ("section", "y", "z")


def dot(a, b):
    return jnp.dot(a, b, preferred_element_type=F32)


def dot_nt(a, b):
    return lax.dot_general(a, b, (((1,), (1,)), ((), ())), preferred_element_type=F32)


def dot_tn(a, b):
    return lax.dot_general(a, b, (((0,), (0,)), ((), ())), preferred_element_type=F32)


def shape_of(*dims, dtype=BF16):
    return jax.ShapeDtypeStruct(dims, dtype)


def in_vmem():
    return pl.BlockSpec(memory_space=pltpu.VMEM)


def in_hbm():
    return pl.BlockSpec(memory_space=pltpu.HBM)


def without(kernel, place):
    def run(*refs):
        kernel(*refs[:place], *refs[place + 1 :])

    return run


def call(kernel, args, outs, *, flops, hbm=0, scratch=(), in_place=False, stay=0, to_hbm=False, after=None):
    stay = len(outs) if stay == 0 else stay
    kept = [pltpu.VMEM(o.shape, o.dtype) for o in outs[stay:]]
    scratch = [*scratch, *kept]
    if kept:
        scratch.append(pltpu.SemaphoreType.DMA((len(kept),)))
    moved = sum(math.prod(o.shape) * o.dtype.itemsize for o in outs)
    moved += sum(math.prod(a.shape) * a.dtype.itemsize for a in args)
    in_specs = [in_hbm() if k < hbm else in_vmem() for k in range(len(args))]
    args = [pltpu.with_memory_space_constraint(a, pltpu.HBM) if k < hbm else a for k, a in enumerate(args)]
    for array in after or ():
        kernel = without(kernel, len(args))
        args = (*args, array)
        in_specs.append(pl.BlockSpec(memory_space=pl.ANY))
    return pl.pallas_call(
        kernel,
        in_specs=in_specs,
        out_specs=[in_hbm() if to_hbm or k >= stay else in_vmem() for k in range(len(outs))],
        out_shape=[pltpu.HBM(o.shape, o.dtype) if to_hbm or k >= stay else o for k, o in enumerate(outs)],
        scratch_shapes=scratch,
        input_output_aliases={0: 0} if in_place else {},
        compiler_params=pltpu.CompilerParams(vmem_limit_bytes=VMEM),
        cost_estimate=pl.CostEstimate(flops=flops, bytes_accessed=min(moved, 16 * 1024 * 1024), transcendentals=0),
    )(*args)


def rows_of(refs):
    return jnp.concatenate([r[...] for r in refs], axis=0)


class Kept:
    def __init__(self, targets, refs):
        self.targets, self.held, self.sems = targets, refs[:-1], refs[-1]
        self.copies = []

    def send(self, k):
        copy = pltpu.make_async_copy(self.held[k], self.targets[k], self.sems.at[k])
        copy.start()
        self.copies.append(copy)

    def wait(self):
        for copy in self.copies:
            copy.wait()


class Loads:
    def __init__(self, sources, held, sems):
        self.held = held
        self.copies = [pltpu.make_async_copy(a, b, sems.at[k]) for k, (a, b) in enumerate(zip(sources, held))]
        for copy in self.copies:
            copy.start()

    def wait(self, *which):
        for k in which:
            self.copies[k].wait()
        return [self.held[k] for k in which]


def loads_of(*arrays):
    return [pltpu.VMEM(a.shape, a.dtype) for a in arrays] + [pltpu.SemaphoreType.DMA((len(arrays),))]


class Weights:
    def __init__(self, source, held, sems, pieces):
        self.held = held
        self.copies = []
        for k, (half, row, count, to) in enumerate(pieces):
            copy = pltpu.make_async_copy(
                source.at[half, :, row : row + count, :], held.at[:, to : to + count, :], sems.at[k]
            )
            copy.start()
            self.copies.append(copy)

    def wait(self, k):
        self.copies[k].wait()

    def tile(self, row, count=TILE):
        return self.held[:, row : row + count, :].reshape(BLOCKS * count, TILE)

    def block(self, b, row):
        return self.held[b, row : row + TILE, :]


def lane_head(width, of):
    lane = lax.broadcasted_iota(jnp.int32, (128, TILE), 1)
    return (lane // width) % 4 == of


def stacked(array, width):
    zero = jnp.zeros((), array.dtype)
    return jnp.concatenate([jnp.where(lane_head(width, h), array, zero) for h in range(4)], axis=0)


def unstacked(array, width):
    out = jnp.where(lane_head(width, 0), array[:128], 0.0)
    for h in range(1, 4):
        out = jnp.where(lane_head(width, h), array[128 * h : 128 * (h + 1)], out)
    return out


def twisted(u, table_ref, sign):
    def wide(k):
        t = table_ref[k]
        return jnp.concatenate([t, t], axis=1)

    n = u.shape[1]
    half = ROT // 2
    side = pltpu.roll(u, n - half, 1) * wide(1) + pltpu.roll(u, half, 1) * wide(2)
    return u * wide(0) + (side if sign > 0 else -side)


def probabilities(qs, k, mask):
    s = dot_nt(qs, k) * HEAD_DIM**-0.5
    s = jnp.where(jnp.concatenate([mask] * 4, axis=0) > 0, s, NEG_FILL)
    e = jnp.exp(s - jnp.max(s, axis=1, keepdims=True))
    return e / jnp.sum(e, axis=1, keepdims=True)


def put_halves(a_ref, b_ref, j, part):
    part = part.astype(BF16)
    a_ref[:, TILE * j : TILE * (j + 1)] = part[:HALF]
    b_ref[:, TILE * j : TILE * (j + 1)] = part[HALF:]


def attention_kernel(w_ref, table_ref, mask_ref, *refs):
    n_refs, (bias_ref, pa_ref, pb_ref), refs = refs[:8], refs[8:11], refs[11:]
    held, sems, loads, kept = refs[5], refs[6], Loads((table_ref, mask_ref), refs[7:9], refs[9]), Kept(refs[:5], refs[10:])
    weights = Weights(w_ref, held, sems, [(t // 2, TILE * (t % 2), TILE, TILE * t) for t in range(4)])
    n_ref, q_ref, k_ref, v_ref, o_ref = kept.held
    n = rows_of(n_refs)
    n_ref[...] = n
    kept.send(0)
    table_ref, mask_ref = loads.wait(0, 1)
    for j, ref in enumerate((q_ref, k_ref, v_ref)):
        weights.wait(j)
        u = dot(n, weights.tile(TILE * j)) + bias_ref[j : j + 1, :]
        ref[...] = (twisted(u, table_ref, 1) if j < 2 else u).astype(BF16)
        kept.send(1 + j)
    for g in range(GROUP // 128):
        rows = slice(128 * g, 128 * g + 128)
        p = probabilities(stacked(q_ref[rows, :], HEAD_DIM), k_ref[rows, :], mask_ref[rows, :])
        o_ref[rows, :] = unstacked(dot(p.astype(BF16), v_ref[rows, :]), 32).astype(BF16)
    kept.send(4)
    o = o_ref[...]
    weights.wait(3)
    for j in range(BLOCKS):
        put_halves(pa_ref, pb_ref, j, dot(o, weights.tile(3 * TILE + 32 * j, 32)))
    kept.wait()


def attention(after, weights, blocks, bias, table, mask):
    return call(
        attention_kernel,
        (weights, table, mask, *blocks, bias),
        [shape_of(HALF, D), shape_of(HALF, D), shape_of(GROUP, D)] + [shape_of(GROUP, TILE)] * 4,
        hbm=3,
        stay=2,
        after=after,
        flops=2 * GROUP * D * 4 * TILE,
        scratch=[pltpu.VMEM((BLOCKS, 4 * TILE, TILE), BF16), pltpu.SemaphoreType.DMA((4,))] + loads_of(table, mask),
    )


def feed_pieces():
    first = []
    for j in range(3):
        first.append((0, ATTN + TILE * j, TILE, TILE * j))
        first.append((1, ATTN + TILE * j, TILE, TILE * (3 + j)))
    last = [(h, ATTN + 3 * TILE, 4 * PADDED, 6 * TILE + 4 * PADDED * h) for h in range(2)]
    return first, last


FEED_SCRATCH = (BLOCKS, 9 * TILE, TILE)


def feed_kernel(w_ref, *refs):
    n_refs, (pa_ref, pb_ref), refs = refs[:8], refs[8:10], refs[10:]
    held, sems, kept = refs[4], refs[5], Kept(refs[:4], refs[6:])
    first, last = feed_pieces()
    weights = Weights(w_ref, held, sems, first + last)
    n_ref, g_ref, u_ref, act_ref = kept.held
    n = rows_of(n_refs)
    n_ref[...] = n
    kept.send(0)
    for j in range(3):
        lanes = slice(TILE * j, TILE * (j + 1))
        weights.wait(2 * j)
        g = dot(n, weights.tile(TILE * j))
        weights.wait(2 * j + 1)
        u = dot(n, weights.tile(TILE * (3 + j)))
        g_ref[:, lanes] = g
        u_ref[:, lanes] = u
        act_ref[:, lanes] = (g * jax.nn.sigmoid(g) * u).astype(BF16)
    for k in range(1, 4):
        kept.send(k)
    act = act_ref[...]
    for j in range(BLOCKS):
        if j % 4 == 0:
            weights.wait(6 + j // 4)
        put_halves(pa_ref, pb_ref, j, dot(act, weights.tile(6 * TILE + PADDED * j, PADDED)))
    kept.wait()


def feed(after, weights, blocks):
    return call(
        feed_kernel,
        (weights, *blocks),
        [shape_of(HALF, D), shape_of(HALF, D), shape_of(GROUP, D)]
        + [shape_of(GROUP, WIDE, dtype=F32)] * 2
        + [shape_of(GROUP, WIDE)],
        hbm=1,
        stay=2,
        after=after,
        flops=2 * GROUP * D * 9 * TILE,
        scratch=[pltpu.VMEM(FEED_SCRATCH, BF16), pltpu.SemaphoreType.DMA((8,))],
    )


def feed_back_kernel(w_ref, g_ref, u_ref, *refs):
    m_refs, (ea_ref, eb_ref), refs = refs[:8], refs[8:10], refs[10:]
    held, sems, loads, kept = refs[3], refs[4], Loads((g_ref, u_ref), refs[5:7], refs[7]), Kept(refs[:3], refs[8:])
    first, last = feed_pieces()
    weights = Weights(w_ref, held, sems, last + first)
    m_ref, dg_ref, du_ref = kept.held
    gm = rows_of(m_refs)
    m_ref[...] = gm
    kept.send(0)
    da = jnp.zeros((GROUP, WIDE), F32)
    for j in range(BLOCKS):
        if j % 4 == 0:
            weights.wait(j // 4)
        da += dot_nt(gm[:, TILE * j : TILE * (j + 1)], weights.tile(6 * TILE + PADDED * j, PADDED))
    g, u = [ref[...] for ref in loads.wait(0, 1)]
    sigma = jax.nn.sigmoid(g)
    dg_ref[...] = (da * u * sigma * (1.0 + g * (1.0 - sigma))).astype(BF16)
    du_ref[...] = (da * g * sigma).astype(BF16)
    kept.send(1)
    kept.send(2)
    dg = dg_ref[...]
    du = du_ref[...]
    for k in range(6):
        weights.wait(2 + k)
    for b in range(BLOCKS):
        e = jnp.zeros((GROUP, TILE), F32)
        for j in range(3):
            lanes = slice(TILE * j, TILE * (j + 1))
            e += dot_nt(dg[:, lanes], weights.block(b, TILE * j))
            e += dot_nt(du[:, lanes], weights.block(b, TILE * (3 + j)))
        put_halves(ea_ref, eb_ref, b, e)
    kept.wait()


def feed_back(after, weights, blocks, g, u):
    return call(
        feed_back_kernel,
        (weights, g, u, *blocks),
        [shape_of(HALF, D), shape_of(HALF, D), shape_of(GROUP, D)] + [shape_of(GROUP, WIDE)] * 2,
        hbm=3,
        stay=2,
        after=after,
        flops=2 * GROUP * D * 9 * TILE,
        scratch=[pltpu.VMEM(FEED_SCRATCH, BF16), pltpu.SemaphoreType.DMA((8,))] + loads_of(g, u),
    )


def attention_back_kernel(w_ref, *refs):
    sources, d_refs, (ea_ref, eb_ref, sum_ref), refs = refs[:5], refs[5:13], refs[13:16], refs[16:]
    held, sems, loads, kept = refs[4], refs[5], Loads(sources, refs[6:11], refs[11]), Kept(refs[:4], refs[12:])
    d_ref, dq_ref, dk_ref, dv_ref = kept.held
    order = (3, 0, 1, 2)
    weights = Weights(w_ref, held, sems, [(t // 2, TILE * (t % 2), TILE, TILE * t) for t in order])
    dattn = rows_of(d_refs)
    d_ref[...] = dattn
    kept.send(0)
    weights.wait(0)
    do = jnp.zeros((GROUP, TILE), F32)
    for j in range(BLOCKS):
        do += dot_nt(dattn[:, TILE * j : TILE * (j + 1)], weights.tile(3 * TILE + 32 * j, 32))
    do = do.astype(BF16)
    q_ref, k_ref, v_ref, table_ref, mask_ref = loads.wait(*range(5))
    dqs, dks = [], []
    for g in range(GROUP // 128):
        rows = slice(128 * g, 128 * g + 128)
        qs = stacked(q_ref[rows, :], HEAD_DIM)
        k = k_ref[rows, :]
        p = probabilities(qs, k, mask_ref[rows, :])
        dos = stacked(do[rows], 32)
        dp = dot_nt(dos, v_ref[rows, :])
        ds = (p * (dp - jnp.sum(p * dp, axis=1, keepdims=True))).astype(BF16)
        dv_ref[rows, :] = dot_tn(p.astype(BF16), dos).astype(BF16)
        dqs.append(unstacked(dot(ds, k), HEAD_DIM))
        dks.append(dot_tn(ds, qs))
    factor = HEAD_DIM**-0.5
    dq_ref[...] = twisted(jnp.concatenate(dqs, axis=0) * factor, table_ref, -1).astype(BF16)
    dk_ref[...] = twisted(jnp.concatenate(dks, axis=0) * factor, table_ref, -1).astype(BF16)
    for k in range(1, 4):
        kept.send(k)
    parts = (dq_ref[...], dk_ref[...], dv_ref[...])
    sums = [jnp.sum(part.astype(F32), axis=0, keepdims=True) for part in parts]
    sum_ref[...] = jnp.concatenate(sums + [jnp.zeros((5, TILE), F32)], axis=0)
    for j in range(3):
        weights.wait(1 + j)
    for b in range(BLOCKS):
        e = jnp.zeros((GROUP, TILE), F32)
        for j in range(3):
            e += dot_nt(parts[j], weights.block(b, TILE * j))
        put_halves(ea_ref, eb_ref, b, e)
    kept.wait()


def attention_back(after, weights, blocks, q, k, v, table, mask):
    return call(
        attention_back_kernel,
        (weights, q, k, v, table, mask, *blocks),
        [shape_of(HALF, D), shape_of(HALF, D), shape_of(8, TILE, dtype=F32), shape_of(GROUP, D)]
        + [shape_of(GROUP, TILE)] * 3,
        hbm=6,
        stay=3,
        after=after,
        flops=2 * GROUP * D * 4 * TILE,
        scratch=[pltpu.VMEM((BLOCKS, 4 * TILE, TILE), BF16), pltpu.SemaphoreType.DMA((4,))] + loads_of(q, k, v, table, mask),
    )


def send_out(copies, source, target, sem):
    copy = pltpu.make_async_copy(source, target, sem)
    copy.start()
    copies.append(copy)


def feed_grads_kernel(row, *refs):
    sources, (vec_ref, out_ref, held, sems), refs = refs[:5], refs[5:9], refs[9:]
    loads = Loads(sources, refs[:5], refs[5])
    copies = []
    n, dg, du = [ref[...] for ref in loads.wait(0, 1, 2)]
    for b in range(BLOCKS):
        left = n[:, TILE * b : TILE * (b + 1)]
        for half, right in enumerate((dg, du)):
            for j in range(3):
                lanes = slice(TILE * j, TILE * (j + 1))
                held[half, b, lanes, :] = dot_tn(left, right[:, lanes]).astype(BF16)
    act, gm = [ref[...] for ref in loads.wait(3, 4)]
    for j in range(BLOCKS):
        half, k = divmod(j, 4)
        part = dot_tn(act, gm[:, TILE * j : TILE * (j + 1)]).astype(BF16)
        at = 3 * TILE + PADDED * k
        held[half, :, at : at + PADDED, :] = part.reshape(BLOCKS, PADDED, TILE)
    send_out(copies, held, out_ref.at[:, :, row : row + FEED, :], sems.at[0])
    send_out(copies, vec_ref, out_ref.at[:, :, row + FEED : row + FEED + VEC, :], sems.at[1])
    for copy in copies:
        copy.wait()


def feed_grads(after, n, dg, du, act, gm, vec):
    return call(
        functools.partial(feed_grads_kernel, 0),
        (n, dg, du, act, gm, vec),
        [shape_of(2, BLOCKS, SUMS, TILE)],
        hbm=5,
        after=after,
        flops=2 * GROUP * D * 9 * TILE,
        scratch=[pltpu.VMEM((2, BLOCKS, FEED, TILE), BF16), pltpu.SemaphoreType.DMA((2,))] + loads_of(n, dg, du, act, gm),
        to_hbm=True,
    )[0]


def attention_grads_kernel(row, *refs):
    sources, (vec_ref, out_ref, held, sems), refs = refs[:6], refs[6:10], refs[10:]
    loads = Loads(sources, refs[:6], refs[6])
    copies = []
    n, dq, dk, dv = [ref[...] for ref in loads.wait(0, 3, 4, 5)]
    for b in range(BLOCKS):
        left = n[:, TILE * b : TILE * (b + 1)]
        for j, right in enumerate((dq, dk, dv)):
            half, at = divmod(TILE * j, ATTN)
            held[half, b, at : at + TILE, :] = dot_tn(left, right).astype(BF16)
    dattn, o = [ref[...] for ref in loads.wait(1, 2)]
    for j in range(BLOCKS):
        part = dot_tn(o, dattn[:, TILE * j : TILE * (j + 1)]).astype(BF16)
        held[1, :, TILE + 32 * j : TILE + 32 * (j + 1), :] = part.reshape(BLOCKS, 32, TILE)
    send_out(copies, held, out_ref.at[:, :, row : row + ATTN, :], sems.at[0])
    send_out(copies, vec_ref, out_ref.at[:, :, row + ATTN : row + ATTN + VEC, :], sems.at[1])
    for copy in copies:
        copy.wait()


def attention_grads(after, sums, n, dattn, o, dq, dk, dv, vec):
    return call(
        without(functools.partial(attention_grads_kernel, FEED + VEC), 0),
        (sums, n, dattn, o, dq, dk, dv, vec),
        [shape_of(2, BLOCKS, SUMS, TILE)],
        hbm=7,
        in_place=True,
        after=after,
        flops=2 * GROUP * D * 4 * TILE,
        scratch=[pltpu.VMEM((2, BLOCKS, ATTN, TILE), BF16), pltpu.SemaphoreType.DMA((2,))] + loads_of(n, dattn, o, dq, dk, dv),
        to_hbm=True,
    )[0]


def add_kernel(a_ref, b_ref, first_ref, *refs):
    for k, ref in enumerate((first_ref, *refs)):
        rows = slice(ROWS * k, ROWS * (k + 1))
        ref[...] = (a_ref[rows, :].astype(F32) + b_ref[rows, :].astype(F32)).astype(ref.dtype)


def added(after, a, b):
    return call(
        add_kernel,
        (a, b),
        [shape_of(ROWS, D, dtype=F32)] + [shape_of(ROWS, D)] * 3,
        flops=HALF * D,
        after=after,
    )


def total_of(refs):
    total = refs[0][...]
    for ref in refs[1:]:
        total = total + ref[...].astype(F32)
    return total


def unit_of(values):
    mean = jnp.mean(values, axis=-1, keepdims=True)
    centred = values - mean
    scale = lax.rsqrt(jnp.mean(centred * centred, axis=-1, keepdims=True) + EPSILON)
    return centred * scale, scale


def norm_kernel(row, base_ref, *refs):
    parts, (gain_ref, out_ref, n_ref) = refs[:4], refs[4:]
    out = (base_ref[...].astype(F32) + total_of(parts)).astype(out_ref.dtype)
    out_ref[...] = out
    unit, _ = unit_of(out.astype(F32))
    n_ref[...] = (unit * gain_ref[row : row + 1, :] + gain_ref[row + 1 : row + 2, :]).astype(BF16)


def normed(after, base, parts, gains, row, dtype):
    return call(
        functools.partial(norm_kernel, row),
        (base, *parts, gains),
        [shape_of(ROWS, D, dtype=dtype), shape_of(ROWS, D)],
        flops=16 * ROWS * D,
        after=after,
    )


def norm_back_kernel(row, up_ref, *refs):
    parts, (values_ref, gain_ref, grad_ref, low_ref, sum_ref) = refs[:4], refs[4:]
    e = total_of(parts)
    unit, scale = unit_of(values_ref[...].astype(F32))
    q = e * gain_ref[row : row + 1, :]
    back = scale * (q - jnp.mean(q, axis=-1, keepdims=True) - unit * jnp.mean(q * unit, axis=-1, keepdims=True))
    grad = up_ref[...].astype(F32) + back
    grad_ref[...] = grad
    low_ref[...] = grad.astype(BF16)
    sums = [jnp.sum(e * unit, axis=0, keepdims=True), jnp.sum(e, axis=0, keepdims=True)]
    sum_ref[...] = jnp.concatenate(sums + [jnp.zeros((6, D), F32)], axis=0)


def normed_back(after, up, parts, values, gains, row):
    return call(
        functools.partial(norm_back_kernel, row),
        (up, *parts, values, gains),
        [shape_of(ROWS, D, dtype=F32), shape_of(ROWS, D), shape_of(8, D, dtype=F32)],
        flops=32 * ROWS * D,
        after=after,
    )


def feed_both_kernel(w_ref, *refs):
    m_refs, n_refs = refs[:8], refs[8:16]
    pa_ref, pb_ref, ea_ref, eb_ref, *refs = refs[16:]
    held, sems, kept = refs[5], refs[6], Kept(refs[:5], (*refs[8:13], refs[13]))
    n_ref, m_ref, act_ref, dg_ref, du_ref = kept.held
    loads = Loads(m_refs, [m_ref.at[ROWS * k : ROWS * (k + 1), :] for k in range(8)], refs[7])
    first, last = feed_pieces()
    weights = Weights(w_ref, held, sems, last + first)
    n = rows_of(n_refs)
    n_ref[...] = n
    kept.send(0)
    loads.wait(*range(8))
    gm = m_ref[...]
    kept.send(1)
    weights.wait(0)
    weights.wait(1)
    for j in range(3):
        lanes = slice(TILE * j, TILE * (j + 1))
        weights.wait(2 + 2 * j)
        g = dot(n, weights.tile(TILE * j))
        weights.wait(3 + 2 * j)
        u = dot(n, weights.tile(TILE * (3 + j)))
        da = jnp.zeros((GROUP, TILE), F32)
        for b in range(BLOCKS):
            w = weights.tile(6 * TILE + PADDED * b, PADDED)[lanes]
            da += dot_nt(gm[:, TILE * b : TILE * (b + 1)], w)
        sigma = jax.nn.sigmoid(g)
        act_ref[:, lanes] = (g * sigma * u).astype(BF16)
        dg_ref[:, lanes] = (da * u * sigma * (1.0 + g * (1.0 - sigma))).astype(BF16)
        du_ref[:, lanes] = (da * g * sigma).astype(BF16)
    for k in range(2, 5):
        kept.send(k)
    act = act_ref[...]
    dg = dg_ref[...]
    du = du_ref[...]
    for b in range(BLOCKS):
        e = jnp.zeros((GROUP, TILE), F32)
        for j in range(3):
            lanes = slice(TILE * j, TILE * (j + 1))
            e += dot_nt(dg[:, lanes], weights.block(b, TILE * j))
            e += dot_nt(du[:, lanes], weights.block(b, TILE * (3 + j)))
        put_halves(ea_ref, eb_ref, b, e)
        put_halves(pa_ref, pb_ref, b, dot(act, weights.tile(6 * TILE + PADDED * b, PADDED)))
    kept.wait()


def feed_both(after, weights, blocks, top):
    return call(
        feed_both_kernel,
        (weights, *top, *blocks),
        [shape_of(HALF, D)] * 4 + [shape_of(GROUP, D)] * 2 + [shape_of(GROUP, WIDE)] * 3,
        hbm=9,
        stay=4,
        after=after,
        flops=4 * GROUP * D * 9 * TILE,
        scratch=[pltpu.VMEM(FEED_SCRATCH, BF16), pltpu.SemaphoreType.DMA((8,)), pltpu.SemaphoreType.DMA((8,))],
    )


def pieces_in_order():
    place = np.zeros((WIDE, 8 * PIECE), np.float32)
    for z in range(4):
        for c in range(2):
            for k in range(PIECE):
                place[(4 * c + z) * PADDED + k, (2 * z + c) * PIECE + k] = 1.0
    return jnp.asarray(place, BF16)


def values_in_order():
    place = np.zeros((TILE, TILE), np.float32)
    for head in range(4):
        for half in range(2):
            for k in range(32):
                place[(half * 4 + head) * 32 + k, (head * 2 + half) * 32 + k] = 1.0
    return jnp.asarray(place, BF16)


def columns_of(ref, b):
    return jnp.concatenate([ref[:, 64 * (8 * x + b) : 64 * (8 * x + b + 1)] for x in range(4)], axis=1)


def pack_rows_kernel(out_in, down_in, low_ref, high_ref, out_ref, down_ref, sems):
    Loads((out_in, down_in), (out_ref, down_ref), sems).wait(0, 1)
    pad = jnp.zeros((PADDED - PIECE, TILE), BF16)
    for b in range(BLOCKS):
        high_ref[32 * b : 32 * (b + 1), :] = columns_of(out_ref, b)
        down = jnp.concatenate([columns_of(down_ref, b), pad], axis=0)
        row = PADDED * (b % 4)
        if b < 4:
            low_ref[row : row + PADDED, :] = down
        else:
            high_ref[TILE + row : TILE + row + PADDED, :] = down
    low_ref[DOWN:, :] = jnp.zeros((TILE, TILE), BF16)


def packed_rows(out_weight, down_weight):
    return call(
        pack_rows_kernel,
        (out_weight, down_weight),
        [shape_of(DOWN + TILE, TILE), shape_of(DOWN + TILE, TILE)],
        hbm=2,
        scratch=loads_of(out_weight, down_weight),
        flops=1024,
    )


def pack_kernel(qkv_in, gate_in, places_in, values_in, cut_ref, *refs):
    loads = Loads((gate_in, places_in, qkv_in, values_in), refs[:4], refs[4])
    wide = 8 * PIECE
    gate_ref, places_ref = loads.wait(0, 1)
    rows = jnp.concatenate([gate_ref[:, wide * k : wide * (k + 1)] for k in range(16)], axis=0)
    placed = dot_nt(rows, places_ref[...]).astype(BF16)
    qkv_ref, values_ref = loads.wait(2, 3)
    values = jnp.concatenate([qkv_ref[:, 2 * D + TILE * t : 2 * D + TILE * (t + 1)] for t in range(8)], axis=0)
    values = dot_nt(values, values_ref[...]).astype(BF16)
    for t in range(8):
        cut_ref[0, t, 0] = qkv_ref[:, TILE * t : TILE * (t + 1)]
        cut_ref[0, t, 1] = qkv_ref[:, D + TILE * t : D + TILE * (t + 1)]
        cut_ref[1, t, 0] = values[32 * t : 32 * (t + 1)]
        cut_ref[1, t, 4] = jnp.zeros((32, TILE), BF16)
        for half in range(2):
            row = 32 * (8 * half + t)
            for j in range(3):
                cut_ref[half, t, 2 - half + j] = placed[row : row + 32, TILE * j : TILE * (j + 1)]


def packed(after, qkv_weight, gate_up):
    places, values = pieces_in_order(), values_in_order()
    return call(
        pack_kernel,
        (qkv_weight, gate_up, places, values),
        [shape_of(2, 8, 5, 32, TILE)],
        hbm=4,
        after=after,
        scratch=loads_of(gate_up, places, qkv_weight, values),
        flops=2 * 512 * WIDE * 8 * PIECE,
    )[0]


def put_columns(ref, blocks):
    for x in range(4):
        lanes = slice(64 * x, 64 * (x + 1))
        for k in range(4):
            pair = jnp.concatenate([blocks[2 * k][:, lanes], blocks[2 * k + 1][:, lanes]], axis=1)
            ref[:, 128 * (4 * x + k) : 128 * (4 * x + k + 1)] = pair.astype(F32)


def in_smem():
    return pl.BlockSpec(memory_space=pltpu.SMEM)


def to_owners_kernel(section_ref, sum_0, sum_1, cut_ref, kept_ref, sent_ref):
    lower = section_ref[0, 0] == 0
    rows = []
    for layer, ref in enumerate((sum_0, sum_1)):
        feed = [ref[TILE * j : TILE * (j + 1), :] for j in range(3)]
        down = ref[3 * TILE : FEED, :]
        attn = [ref[FEED + VEC + TILE * j : FEED + VEC + TILE * (j + 1), :] for j in range(2)]
        vecs = [ref[row : row + VEC, :].astype(F32) for row in (FEED + VEC + ATTN, FEED)]
        pad = jnp.zeros((30, TILE), F32)
        vec = [jnp.concatenate([v[o : o + 1] for v in vecs] + [pad], axis=0).astype(BF16) for o in range(8)]
        low = (attn[0], attn[1], feed[0], feed[1], feed[2])
        high = (attn[0], feed[0], feed[1], feed[2], jnp.concatenate(vec, axis=0))
        for t in range(5):
            tile = jnp.where(lower, low[t], high[t])
            for o in range(8):
                cut_ref[layer, o, t] = tile[32 * o : 32 * (o + 1)]
        rows.append((jnp.concatenate([down, attn[1]], axis=0), jnp.concatenate([attn[1], down], axis=0)))
    kept_ref[...] = jnp.where(lower, rows[0][0], rows[1][1])
    sent_ref[...] = jnp.where(lower, rows[1][0], rows[0][1])


def to_owners(after, section, sum_0, sum_1):
    kernel = to_owners_kernel
    for _ in after:
        kernel = without(kernel, 3)
    return pl.pallas_call(
        kernel,
        in_specs=[in_smem(), in_vmem(), in_vmem()] + [pl.BlockSpec(memory_space=pl.ANY)] * len(after),
        out_specs=[in_vmem()] * 3,
        out_shape=[shape_of(2, 8, 5, 32, TILE), shape_of(DOWN + TILE, TILE), shape_of(DOWN + TILE, TILE)],
        compiler_params=pltpu.CompilerParams(vmem_limit_bytes=VMEM),
    )(section, sum_0, sum_1, *after)


def unpack_kernel(section_ref, kept_ref, sent_ref, places_ref, values_ref, cut_ref, qkv_ref, gate_ref, out_ref, down_ref, vec_ref):
    lower = section_ref[0, 0] == 0
    first = jnp.where(lower, kept_ref[:DOWN, :], sent_ref[:DOWN, :])
    second = jnp.where(lower, sent_ref[...], kept_ref[...])
    put_columns(out_ref, [second[32 * b : 32 * (b + 1)] for b in range(BLOCKS)])
    down = []
    for b in range(BLOCKS):
        row = PADDED * (b % 4)
        part = first[row : row + PADDED] if b < 4 else second[TILE + row : TILE + row + PADDED]
        down.append(part.astype(F32)[:PIECE])
    put_columns(down_ref, down)
    wide = 8 * PIECE
    vec = jnp.zeros((8, TILE), F32)
    for t in range(8):
        qkv_ref[:, TILE * t : TILE * (t + 1)] = cut_ref[0, t, 0].astype(F32)
        qkv_ref[:, D + TILE * t : D + TILE * (t + 1)] = cut_ref[0, t, 1].astype(F32)
        qkv_ref[:, 2 * D + TILE * t : 2 * D + TILE * (t + 1)] = dot(cut_ref[1, t, 0], values_ref[...])
        vec += cut_ref[1, t, 4].astype(F32)[:8]
    vec_ref[...] = vec
    rows = [
        jnp.concatenate([cut_ref[half, t, 2 - half + j] for j in range(3)], axis=1) for half in range(2) for t in range(8)
    ]
    placed = dot(jnp.concatenate(rows, axis=0), places_ref[...])
    for k in range(16):
        gate_ref[:, wide * k : wide * (k + 1)] = placed[32 * k : 32 * (k + 1)]


def unpacked(section, kept, sent, cut):
    return pl.pallas_call(
        unpack_kernel,
        in_specs=[in_smem()] + [in_vmem()] * 5,
        out_specs=[in_vmem()] * 5,
        out_shape=[
            shape_of(32, 3 * D, dtype=F32),
            shape_of(32, 2 * FF, dtype=F32),
            shape_of(32, D, dtype=F32),
            shape_of(PIECE, D, dtype=F32),
            shape_of(8, TILE, dtype=F32),
        ],
        compiler_params=pltpu.CompilerParams(vmem_limit_bytes=VMEM),
    )(section, kept, sent, pieces_in_order(), values_in_order(), cut)


def turned(block, axis, step):
    n = math.prod(lax.axis_size(a) for a in (axis if isinstance(axis, tuple) else (axis,)))
    return lax.ppermute(block, axis, [(i, (i - step) % n) for i in range(n)])


def in_order(block, axis, n):
    ahead = jnp.stack([block] + [turned(block, axis, k) for k in range(1, n)])
    return jnp.roll(ahead, lax.axis_index(axis), axis=0)


def gathered_rows(block):
    own = [block] + [turned(block, "x", k) for k in range(1, 4)]
    return own + [turned(part, "core", 1) for part in own]


def summed_parts(after, part_a, part_b):
    first, *rest = added(after, part_a, turned(part_b, "core", 1))
    return [first] + [turned(block, "x", -k) for k, block in enumerate(rest, 1)]


def swapped(block, step):
    pairs = []
    for k in range(2):
        for y in range(2):
            for c in range(2):
                pairs.append((4 * k + 2 * y + c, 4 * ((k + step) % 2) + 2 * c + y))
    return lax.ppermute(block, ("section", "y", "core"), pairs)


def spread(block):
    return lax.all_to_all(block, ("section", "x", "core"), 0, 0, tiled=True)


def scattered(array):
    array = array.reshape(16, -1, TILE)
    return lax.optimization_barrier(lax.psum_scatter(array, SPREAD, scatter_dimension=0, tiled=False))


def to_stored(rows):
    shape = rows.shape[:-1]
    k = len(shape)
    cut = rows.reshape(*shape, 4, 8, 64)
    return jnp.swapaxes(cut, k, k + 1).reshape(*shape, D)


def from_stored(rows):
    shape = rows.shape[:-1]
    k = len(shape)
    cut = rows.reshape(*shape, 8, 4, 64)
    return jnp.swapaxes(cut, k, k + 1).reshape(*shape, D)


def value_columns(cut):
    shape = cut.shape[:-1]
    k = len(shape)
    return jnp.swapaxes(cut.reshape(*shape, 4, 2, 32), k, k + 1).reshape(*shape, TILE)


def value_columns_back(cut):
    shape = cut.shape[:-1]
    k = len(shape)
    return jnp.swapaxes(cut.reshape(*shape, 2, 4, 32), k, k + 1).reshape(*shape, TILE)


def both_layers(qkv_weight, out_weight, gate_up, down_weight):
    section = lax.axis_index("section")
    low, high = packed_rows(out_weight, down_weight)
    cut = spread(packed((low,), qkv_weight, gate_up).reshape(16, 5, 32, TILE))
    cut = cut.reshape(2, 8, 5, 32, TILE).transpose(0, 2, 1, 3, 4).reshape(2, 5 * TILE, TILE)
    kept = swapped(jnp.where(section == 0, low, high), 0)
    sent = swapped(jnp.where(section == 0, high, low), 1)
    parts = []
    for layer in range(2):
        rows = jnp.where(section == layer, kept, sent)
        low = jnp.concatenate([cut[layer], rows[:DOWN]], axis=0)
        high = jnp.concatenate([cut[layer, :TILE], rows[:TILE], cut[layer, TILE : 4 * TILE], rows[TILE:]], axis=0)
        parts.append(jnp.where(section == 0, low, high))
    return parts


def owned(after, sum_0, sum_1):
    section = lax.axis_index("section").reshape(1, 1)
    cut, kept, sent = to_owners(after, section, sum_0, sum_1)
    kept, sent = swapped(kept, 0), swapped(sent, 1)
    cut = spread(cut.reshape(16, 5, 32, TILE)).reshape(2, 8, 5, 32, TILE)
    return unpacked(section, kept, sent, cut)


def geometry(segments):
    groups = segments.reshape(GROUP // 128, 128)
    index = jnp.arange(128, dtype=jnp.int32)
    block = index // 32
    same = (groups[:, :, None] == groups[:, None, :]) & (block[None, :, None] == block[None, None, :])
    before = index[None, :] < index[:, None]
    places = jnp.sum(jnp.where(same & before, 1.0, 0.0), axis=-1).astype(F32).reshape(GROUP)
    inverse = 10000.0 ** (-(jnp.arange(ROT // 2).astype(F32) * 2.0 / ROT))
    theta = places[:, None] * inverse
    cosine, sine = jnp.cos(theta), jnp.sin(theta)
    rest = HEAD_DIM - ROT
    zero = jnp.zeros((GROUP, ROT // 2), F32)
    straight = jnp.concatenate([cosine, cosine, jnp.ones((GROUP, rest), F32)], axis=1)
    first = jnp.concatenate([-sine, zero, jnp.zeros((GROUP, rest), F32)], axis=1)
    second = jnp.concatenate([zero, sine, jnp.zeros((GROUP, rest), F32)], axis=1)
    table = jnp.stack([jnp.concatenate([t, t], axis=1) for t in (straight, first, second)])
    linked = same & (index[None, :] <= index[:, None])
    return table, jnp.where(linked, 1.0, 0.0).astype(F32).reshape(GROUP, 128)


def vector_rows(*parts):
    cut = jnp.concatenate(parts, axis=2).astype(BF16)
    cut = jnp.pad(cut, ((0, 0), (0, VEC - 8), (0, TILE - cut.shape[2])))
    return jnp.stack([jnp.zeros_like(cut), cut])


def by_owner(vector):
    return vector.reshape(8, 8, 32)


def on_device(
    block_input,
    segment_ids,
    cotangent,
    first_gain,
    first_shift,
    qkv_weight,
    qkv_bias,
    out_weight,
    second_gain,
    second_shift,
    gate_up,
    down_weight,
):
    section = lax.axis_index("section")
    shard = 2 * lax.axis_index("x") + lax.axis_index("core")

    weights = []
    for part in both_layers(qkv_weight[0], out_weight[0], gate_up[0], down_weight[0]):
        full = lax.all_gather(part, SPREAD, axis=0, tiled=True)
        weights.append(full.reshape(2, BLOCKS, LAYER, TILE))

    vectors = jnp.concatenate([first_gain[0], first_shift[0], second_gain[0], second_shift[0], qkv_bias[0]])
    vectors = jnp.pad(vectors, (0, 32)).reshape(1, TILE)
    vectors = in_order(vectors, "core", 2)
    vectors = in_order(vectors, "x", 4)
    vectors = in_order(vectors, "z", 4)
    vectors = in_order(vectors, RING, 4)
    vectors = vectors.reshape(2, 64, TILE).astype(F32)
    gains = vectors[:, :, :128].reshape(2, 64, 4, 32).transpose(0, 2, 1, 3).reshape(8, D)
    bias = vectors[:, :, 128:224].reshape(2, 2, 4, 4, 2, 96).transpose(0, 3, 1, 2, 4, 5).reshape(2, 3, 8, TILE)
    bias = lax.dynamic_index_in_dim(bias, shard, 2, keepdims=False)
    bias = jnp.concatenate([bias[:, :2], value_columns(bias[:, 2:])], axis=1)
    bias = jnp.pad(bias, ((0, 0), (0, 5), (0, 0)))

    def own_rows(array):
        return lax.dynamic_slice_in_dim(array, 2 * section, 2, 0)

    rows_in = to_stored(own_rows(block_input).reshape(ROWS, D))
    top_grad = to_stored(own_rows(cotangent).reshape(ROWS, D))
    segments = gathered_rows(own_rows(segment_ids).reshape(1, ROWS))
    tables = geometry(jnp.concatenate(segments, axis=0))
    top = gathered_rows(top_grad)
    outputs = [None, None]
    kept = [{}, {}]
    base = rows_in
    unit, _ = unit_of(base.astype(F32))
    n = (unit * gains[0:1] + gains[1:2]).astype(BF16)
    for layer in range(2):
        have = kept[layer]
        part_a, part_b, have["n1"], have["q"], have["k"], have["v"], have["mixed"] = attention(
            top if layer == 0 else None, weights[layer], gathered_rows(n), bias[layer], *tables
        )
        have["values1"] = base
        hidden, n = normed(None, base, summed_parts(None, part_a, part_b), gains, 4 * layer + 2, F32)
        have["values2"] = hidden
        if layer == 0:
            part_a, part_b, have["n2"], have["g"], have["u"], have["act"] = feed(None, weights[0], gathered_rows(n))
            base, n = normed(None, hidden, summed_parts(None, part_a, part_b), gains, 4, BF16)
            outputs[0] = base
    part_a, part_b, ea, eb, have["n2"], have["gm"], have["act"], have["dg"], have["du"] = feed_both(
        None, weights[1], gathered_rows(n), top
    )

    def feed_sums(have):
        sums = have["sums2"]
        vec = vector_rows(by_owner(sums[0]), by_owner(sums[1]))
        return feed_grads(None, have["n2"], have["dg"], have["du"], have["act"], have["gm"], vec)

    def attention_sums(have, buffer):
        sums = have["sums1"]
        bias_sum = have["bias_sum"]
        bias_sum = jnp.concatenate([bias_sum[:2], value_columns_back(bias_sum[2:3])], axis=0)
        bias_sum = lax.dynamic_update_slice_in_dim(jnp.zeros((3, 8, TILE), F32), bias_sum[:, None], shard, 1)
        bias_sum = bias_sum.reshape(4, 2, 4, 2, 96).transpose(1, 2, 0, 3, 4).reshape(8, 8, 96)
        vec = vector_rows(by_owner(sums[0]), by_owner(sums[1]), bias_sum)
        names = ("n1", "dattn", "mixed", "dq", "dk", "dv")
        return attention_grads(None, buffer, *(have[name] for name in names), vec)

    grads_in = [None, None]
    up = top_grad
    sums_1 = None
    for layer in (1, 0):
        have = kept[layer]
        if layer == 0:
            ea, eb, have["gm"], have["dg"], have["du"] = feed_back(
                (sums_1,), weights[0], gathered_rows(up), have["g"], have["u"]
            )
        grad, low, have["sums2"] = normed_back(None, up, summed_parts(None, ea, eb), have["values2"], gains, 4 * layer + 2)
        buffer = feed_sums(have)
        ea, eb, have["bias_sum"], have["dattn"], have["dq"], have["dk"], have["dv"] = attention_back(
            (buffer,), weights[layer], gathered_rows(low), have["q"], have["k"], have["v"], *tables
        )
        parts = summed_parts(None, ea, eb)
        grads_in[layer], up, have["sums1"] = normed_back(None, grad, parts, have["values1"], gains, 4 * layer)
        if layer == 1:
            sums_1 = attention_sums(have, buffer)
    sums_0 = attention_sums(kept[0], buffer)
    first, *rest = summed_parts((sums_0,), part_a, part_b)
    total = kept[1]["values2"] + first
    for block in rest:
        total = total + block.astype(F32)
    outputs[1] = total.astype(BF16)

    sum_1 = scattered(sums_1)
    sum_0 = scattered(sums_0)
    def layer_rows(first, second):
        mine = jnp.where(section == 0, first, second)
        other = turned(jnp.where(section == 0, second, first).astype(BF16), "section", 1).astype(first.dtype)
        rows = jnp.where(section == 0, jnp.concatenate([mine, other]), jnp.concatenate([other, mine]))
        return from_stored(rows).reshape(1, 4, 32, D)

    activations = layer_rows(outputs[0], outputs[1])
    input_grads = layer_rows(grads_in[0], upstream_of(grads_in[1]))
    qkv_grad, gate_up_grad, out_grad, down_grad, small = owned((activations, input_grads), sum_0, sum_1)
    return (
        activations,
        input_grads,
        small[0][None, 0:32],
        small[0][None, 32:64],
        qkv_grad[None],
        small[0][None, 64:160],
        out_grad[None],
        small[1][None, 0:32],
        small[1][None, 32:64],
        gate_up_grad[None],
        down_grad[None],
    )


def upstream_of(grad_rows):
    return grad_rows.astype(BF16).astype(F32)


def solution(mesh):
    grid = Mesh(mesh.devices.reshape(2, 4, 2, 4, 2), GRID)
    return jax.shard_map(
        on_device,
        mesh=grid,
        in_specs=(
            P(None, DP, None),
            P(None, DP),
            P(None, DP, None),
            P("section", DP),
            P("section", DP),
            P("section", DP, None),
            P("section", DP),
            P("section", DP, None),
            P("section", DP),
            P("section", DP),
            P("section", DP, None),
            P("section", DP, None),
        ),
        out_specs=(
            P("section", None, DP, None),
            P("section", None, DP, None),
            P("section", DP),
            P("section", DP),
            P("section", DP, None),
            P("section", DP),
            P("section", DP, None),
            P("section", DP),
            P("section", DP),
            P("section", DP, None),
            P("section", DP, None),
        ),
        check_vma=False,
    )
```

```python
import functools
import math

import jax
import jax.numpy as jnp
import numpy as np
from jax import lax
from jax.experimental import pallas as pl
from jax.experimental.pallas import tpu as pltpu
from jax.sharding import Mesh
from jax.sharding import PartitionSpec as P

D = 2048
HEAD_DIM = 64
ROT = 16
FF = 5632
EPSILON = 1e-05
NEG_FILL = -1e30
TILE = 256
BLOCKS = D // TILE
ROWS = 64
GROUP = 8 * ROWS
HALF = GROUP // 2
PIECE = 88
PADDED = 96
WIDE = 8 * PADDED
DOWN = 4 * PADDED
VEC = 16
ATTN = 2 * TILE
FEED = 3 * TILE + DOWN
LAYER = ATTN + FEED
SUMS = LAYER + 2 * VEC
VMEM = 34 * 1024 * 1024
F32 = jnp.float32
BF16 = jnp.bfloat16

GRID = ("section", "x", "y", "z", "core")
DP = ("x", "y", "z", "core")
RING = ("section", "y")
SPREAD = ("section", "y", "z")


def dot(a, b):
    return jnp.dot(a, b, preferred_element_type=F32)


def dot_nt(a, b):
    return lax.dot_general(a, b, (((1,), (1,)), ((), ())), preferred_element_type=F32)


def dot_tn(a, b):
    return lax.dot_general(a, b, (((0,), (0,)), ((), ())), preferred_element_type=F32)


def shape_of(*dims, dtype=BF16):
    return jax.ShapeDtypeStruct(dims, dtype)


def in_vmem():
    return pl.BlockSpec(memory_space=pltpu.VMEM)


def in_hbm():
    return pl.BlockSpec(memory_space=pltpu.HBM)


def without(kernel, place):
    def run(*refs):
        kernel(*refs[:place], *refs[place + 1 :])

    return run


def call(kernel, args, outs, *, flops, hbm=0, scratch=(), in_place=False, stay=0, to_hbm=False, after=None):
    stay = len(outs) if stay == 0 else stay
    kept = [pltpu.VMEM(o.shape, o.dtype) for o in outs[stay:]]
    scratch = [*scratch, *kept]
    if kept:
        scratch.append(pltpu.SemaphoreType.DMA((len(kept),)))
    moved = sum(math.prod(o.shape) * o.dtype.itemsize for o in outs)
    moved += sum(math.prod(a.shape) * a.dtype.itemsize for a in args)
    in_specs = [in_hbm() if k < hbm else in_vmem() for k in range(len(args))]
    args = [pltpu.with_memory_space_constraint(a, pltpu.HBM) if k < hbm else a for k, a in enumerate(args)]
    for array in after or ():
        kernel = without(kernel, len(args))
        args = (*args, pltpu.with_memory_space_constraint(array, pltpu.HBM))
        in_specs.append(in_hbm())
    return pl.pallas_call(
        kernel,
        in_specs=in_specs,
        out_specs=[in_hbm() if to_hbm or k >= stay else in_vmem() for k in range(len(outs))],
        out_shape=[pltpu.HBM(o.shape, o.dtype) if to_hbm or k >= stay else o for k, o in enumerate(outs)],
        scratch_shapes=scratch,
        input_output_aliases={0: 0} if in_place else {},
        compiler_params=pltpu.CompilerParams(vmem_limit_bytes=VMEM),
        cost_estimate=pl.CostEstimate(flops=flops, bytes_accessed=min(moved, 16 * 1024 * 1024), transcendentals=0),
    )(*args)


def rows_of(refs):
    return jnp.concatenate([r[...] for r in refs], axis=0)


class Kept:
    def __init__(self, targets, refs):
        self.targets, self.held, self.sems = targets, refs[:-1], refs[-1]
        self.copies = []

    def send(self, k):
        copy = pltpu.make_async_copy(self.held[k], self.targets[k], self.sems.at[k])
        copy.start()
        self.copies.append(copy)

    def wait(self):
        for copy in self.copies:
            copy.wait()


class Loads:
    def __init__(self, sources, held, sems):
        self.held = held
        self.copies = [pltpu.make_async_copy(a, b, sems.at[k]) for k, (a, b) in enumerate(zip(sources, held))]
        for copy in self.copies:
            copy.start()

    def wait(self, *which):
        for k in which:
            self.copies[k].wait()
        return [self.held[k] for k in which]


def loads_of(*arrays):
    return [pltpu.VMEM(a.shape, a.dtype) for a in arrays] + [pltpu.SemaphoreType.DMA((len(arrays),))]


class Weights:
    def __init__(self, source, held, sems, pieces):
        self.held = held
        self.copies = []
        for k, (half, row, count, to) in enumerate(pieces):
            copy = pltpu.make_async_copy(
                source.at[half, :, row : row + count, :], held.at[:, to : to + count, :], sems.at[k]
            )
            copy.start()
            self.copies.append(copy)

    def wait(self, k):
        self.copies[k].wait()

    def tile(self, row, count=TILE):
        return self.held[:, row : row + count, :].reshape(BLOCKS * count, TILE)

    def block(self, b, row):
        return self.held[b, row : row + TILE, :]


def lane_head(width, of):
    lane = lax.broadcasted_iota(jnp.int32, (128, TILE), 1)
    return (lane // width) % 4 == of


def stacked(array, width):
    zero = jnp.zeros((), array.dtype)
    return jnp.concatenate([jnp.where(lane_head(width, h), array, zero) for h in range(4)], axis=0)


def unstacked(array, width):
    out = jnp.where(lane_head(width, 0), array[:128], 0.0)
    for h in range(1, 4):
        out = jnp.where(lane_head(width, h), array[128 * h : 128 * (h + 1)], out)
    return out


def twisted(u, table_ref, sign):
    def wide(k):
        t = table_ref[k]
        return jnp.concatenate([t, t], axis=1)

    n = u.shape[1]
    half = ROT // 2
    side = pltpu.roll(u, n - half, 1) * wide(1) + pltpu.roll(u, half, 1) * wide(2)
    return u * wide(0) + (side if sign > 0 else -side)


def probabilities(qs, k, mask):
    s = dot_nt(qs, k) * HEAD_DIM**-0.5
    s = jnp.where(jnp.concatenate([mask] * 4, axis=0) > 0, s, NEG_FILL)
    e = jnp.exp(s - jnp.max(s, axis=1, keepdims=True))
    return e / jnp.sum(e, axis=1, keepdims=True)


def put_halves(a_ref, b_ref, j, part):
    part = part.astype(BF16)
    a_ref[:, TILE * j : TILE * (j + 1)] = part[:HALF]
    b_ref[:, TILE * j : TILE * (j + 1)] = part[HALF:]


def attention_kernel(w_ref, table_ref, mask_ref, *refs):
    n_refs, (bias_ref, pa_ref, pb_ref), refs = refs[:8], refs[8:11], refs[11:]
    held, sems, loads, kept = refs[5], refs[6], Loads((table_ref, mask_ref), refs[7:9], refs[9]), Kept(refs[:5], refs[10:])
    weights = Weights(w_ref, held, sems, [(t // 2, TILE * (t % 2), TILE, TILE * t) for t in range(4)])
    n_ref, q_ref, k_ref, v_ref, o_ref = kept.held
    n = rows_of(n_refs)
    n_ref[...] = n
    kept.send(0)
    table_ref, mask_ref = loads.wait(0, 1)
    for j, ref in enumerate((q_ref, k_ref, v_ref)):
        weights.wait(j)
        u = dot(n, weights.tile(TILE * j)) + bias_ref[j : j + 1, :]
        ref[...] = (twisted(u, table_ref, 1) if j < 2 else u).astype(BF16)
        kept.send(1 + j)
    for g in range(GROUP // 128):
        rows = slice(128 * g, 128 * g + 128)
        p = probabilities(stacked(q_ref[rows, :], HEAD_DIM), k_ref[rows, :], mask_ref[rows, :])
        o_ref[rows, :] = unstacked(dot(p.astype(BF16), v_ref[rows, :]), 32).astype(BF16)
    kept.send(4)
    o = o_ref[...]
    weights.wait(3)
    for j in range(BLOCKS):
        put_halves(pa_ref, pb_ref, j, dot(o, weights.tile(3 * TILE + 32 * j, 32)))
    kept.wait()


def attention(after, weights, blocks, bias, table, mask):
    return call(
        attention_kernel,
        (weights, table, mask, *blocks, bias),
        [shape_of(HALF, D), shape_of(HALF, D), shape_of(GROUP, D)] + [shape_of(GROUP, TILE)] * 4,
        hbm=3,
        stay=2,
        after=after,
        flops=2 * GROUP * D * 4 * TILE,
        scratch=[pltpu.VMEM((BLOCKS, 4 * TILE, TILE), BF16), pltpu.SemaphoreType.DMA((4,))] + loads_of(table, mask),
    )


def feed_pieces():
    first = []
    for j in range(3):
        first.append((0, ATTN + TILE * j, TILE, TILE * j))
        first.append((1, ATTN + TILE * j, TILE, TILE * (3 + j)))
    last = [(h, ATTN + 3 * TILE, 4 * PADDED, 6 * TILE + 4 * PADDED * h) for h in range(2)]
    return first, last


FEED_SCRATCH = (BLOCKS, 9 * TILE, TILE)


def feed_kernel(w_ref, *refs):
    n_refs, (pa_ref, pb_ref), refs = refs[:8], refs[8:10], refs[10:]
    held, sems, kept = refs[4], refs[5], Kept(refs[:4], refs[6:])
    first, last = feed_pieces()
    weights = Weights(w_ref, held, sems, first + last)
    n_ref, g_ref, u_ref, act_ref = kept.held
    n = rows_of(n_refs)
    n_ref[...] = n
    kept.send(0)
    for j in range(3):
        lanes = slice(TILE * j, TILE * (j + 1))
        weights.wait(2 * j)
        g = dot(n, weights.tile(TILE * j))
        weights.wait(2 * j + 1)
        u = dot(n, weights.tile(TILE * (3 + j)))
        g_ref[:, lanes] = g
        u_ref[:, lanes] = u
        act_ref[:, lanes] = (g * jax.nn.sigmoid(g) * u).astype(BF16)
    for k in range(1, 4):
        kept.send(k)
    act = act_ref[...]
    for j in range(BLOCKS):
        if j % 4 == 0:
            weights.wait(6 + j // 4)
        put_halves(pa_ref, pb_ref, j, dot(act, weights.tile(6 * TILE + PADDED * j, PADDED)))
    kept.wait()


def feed(after, weights, blocks):
    return call(
        feed_kernel,
        (weights, *blocks),
        [shape_of(HALF, D), shape_of(HALF, D), shape_of(GROUP, D)]
        + [shape_of(GROUP, WIDE, dtype=F32)] * 2
        + [shape_of(GROUP, WIDE)],
        hbm=1,
        stay=2,
        after=after,
        flops=2 * GROUP * D * 9 * TILE,
        scratch=[pltpu.VMEM(FEED_SCRATCH, BF16), pltpu.SemaphoreType.DMA((8,))],
    )


def feed_back_kernel(w_ref, g_ref, u_ref, *refs):
    m_refs, (ea_ref, eb_ref), refs = refs[:8], refs[8:10], refs[10:]
    held, sems, loads, kept = refs[3], refs[4], Loads((g_ref, u_ref), refs[5:7], refs[7]), Kept(refs[:3], refs[8:])
    first, last = feed_pieces()
    weights = Weights(w_ref, held, sems, last + first)
    m_ref, dg_ref, du_ref = kept.held
    gm = rows_of(m_refs)
    m_ref[...] = gm
    kept.send(0)
    da = jnp.zeros((GROUP, WIDE), F32)
    for j in range(BLOCKS):
        if j % 4 == 0:
            weights.wait(j // 4)
        da += dot_nt(gm[:, TILE * j : TILE * (j + 1)], weights.tile(6 * TILE + PADDED * j, PADDED))
    g, u = [ref[...] for ref in loads.wait(0, 1)]
    sigma = jax.nn.sigmoid(g)
    dg_ref[...] = (da * u * sigma * (1.0 + g * (1.0 - sigma))).astype(BF16)
    du_ref[...] = (da * g * sigma).astype(BF16)
    kept.send(1)
    kept.send(2)
    dg = dg_ref[...]
    du = du_ref[...]
    for k in range(6):
        weights.wait(2 + k)
    for b in range(BLOCKS):
        e = jnp.zeros((GROUP, TILE), F32)
        for j in range(3):
            lanes = slice(TILE * j, TILE * (j + 1))
            e += dot_nt(dg[:, lanes], weights.block(b, TILE * j))
            e += dot_nt(du[:, lanes], weights.block(b, TILE * (3 + j)))
        put_halves(ea_ref, eb_ref, b, e)
    kept.wait()


def feed_back(after, weights, blocks, g, u):
    return call(
        feed_back_kernel,
        (weights, g, u, *blocks),
        [shape_of(HALF, D), shape_of(HALF, D), shape_of(GROUP, D)] + [shape_of(GROUP, WIDE)] * 2,
        hbm=3,
        stay=2,
        after=after,
        flops=2 * GROUP * D * 9 * TILE,
        scratch=[pltpu.VMEM(FEED_SCRATCH, BF16), pltpu.SemaphoreType.DMA((8,))] + loads_of(g, u),
    )


def attention_back_kernel(w_ref, *refs):
    sources, d_refs, (ea_ref, eb_ref, sum_ref), refs = refs[:5], refs[5:13], refs[13:16], refs[16:]
    held, sems, loads, kept = refs[4], refs[5], Loads(sources, refs[6:11], refs[11]), Kept(refs[:4], refs[12:])
    d_ref, dq_ref, dk_ref, dv_ref = kept.held
    order = (3, 0, 1, 2)
    weights = Weights(w_ref, held, sems, [(t // 2, TILE * (t % 2), TILE, TILE * t) for t in order])
    dattn = rows_of(d_refs)
    d_ref[...] = dattn
    kept.send(0)
    weights.wait(0)
    do = jnp.zeros((GROUP, TILE), F32)
    for j in range(BLOCKS):
        do += dot_nt(dattn[:, TILE * j : TILE * (j + 1)], weights.tile(3 * TILE + 32 * j, 32))
    do = do.astype(BF16)
    q_ref, k_ref, v_ref, table_ref, mask_ref = loads.wait(*range(5))
    dqs, dks = [], []
    for g in range(GROUP // 128):
        rows = slice(128 * g, 128 * g + 128)
        qs = stacked(q_ref[rows, :], HEAD_DIM)
        k = k_ref[rows, :]
        p = probabilities(qs, k, mask_ref[rows, :])
        dos = stacked(do[rows], 32)
        dp = dot_nt(dos, v_ref[rows, :])
        ds = (p * (dp - jnp.sum(p * dp, axis=1, keepdims=True))).astype(BF16)
        dv_ref[rows, :] = dot_tn(p.astype(BF16), dos).astype(BF16)
        dqs.append(unstacked(dot(ds, k), HEAD_DIM))
        dks.append(dot_tn(ds, qs))
    factor = HEAD_DIM**-0.5
    dq_ref[...] = twisted(jnp.concatenate(dqs, axis=0) * factor, table_ref, -1).astype(BF16)
    dk_ref[...] = twisted(jnp.concatenate(dks, axis=0) * factor, table_ref, -1).astype(BF16)
    for k in range(1, 4):
        kept.send(k)
    parts = (dq_ref[...], dk_ref[...], dv_ref[...])
    sums = [jnp.sum(part.astype(F32), axis=0, keepdims=True) for part in parts]
    sum_ref[...] = jnp.concatenate(sums + [jnp.zeros((5, TILE), F32)], axis=0)
    for j in range(3):
        weights.wait(1 + j)
    for b in range(BLOCKS):
        e = jnp.zeros((GROUP, TILE), F32)
        for j in range(3):
            e += dot_nt(parts[j], weights.block(b, TILE * j))
        put_halves(ea_ref, eb_ref, b, e)
    kept.wait()


def attention_back(after, weights, blocks, q, k, v, table, mask):
    return call(
        attention_back_kernel,
        (weights, q, k, v, table, mask, *blocks),
        [shape_of(HALF, D), shape_of(HALF, D), shape_of(8, TILE, dtype=F32), shape_of(GROUP, D)]
        + [shape_of(GROUP, TILE)] * 3,
        hbm=6,
        stay=3,
        after=after,
        flops=2 * GROUP * D * 4 * TILE,
        scratch=[pltpu.VMEM((BLOCKS, 4 * TILE, TILE), BF16), pltpu.SemaphoreType.DMA((4,))] + loads_of(q, k, v, table, mask),
    )


def send_out(copies, source, target, sem):
    copy = pltpu.make_async_copy(source, target, sem)
    copy.start()
    copies.append(copy)


def feed_grads_kernel(row, *refs):
    sources, (vec_ref, out_ref, held, sems), refs = refs[:5], refs[5:9], refs[9:]
    loads = Loads(sources, refs[:5], refs[5])
    copies = []
    n, dg, du = [ref[...] for ref in loads.wait(0, 1, 2)]
    for b in range(BLOCKS):
        left = n[:, TILE * b : TILE * (b + 1)]
        for half, right in enumerate((dg, du)):
            for j in range(3):
                lanes = slice(TILE * j, TILE * (j + 1))
                held[half, b, lanes, :] = dot_tn(left, right[:, lanes]).astype(BF16)
    act, gm = [ref[...] for ref in loads.wait(3, 4)]
    for j in range(BLOCKS):
        half, k = divmod(j, 4)
        part = dot_tn(act, gm[:, TILE * j : TILE * (j + 1)]).astype(BF16)
        at = 3 * TILE + PADDED * k
        held[half, :, at : at + PADDED, :] = part.reshape(BLOCKS, PADDED, TILE)
    send_out(copies, held, out_ref.at[:, :, row : row + FEED, :], sems.at[0])
    send_out(copies, vec_ref, out_ref.at[:, :, row + FEED : row + FEED + VEC, :], sems.at[1])
    for copy in copies:
        copy.wait()


def feed_grads(after, n, dg, du, act, gm, vec):
    return call(
        functools.partial(feed_grads_kernel, 0),
        (n, dg, du, act, gm, vec),
        [shape_of(2, BLOCKS, SUMS, TILE)],
        hbm=5,
        after=after,
        flops=2 * GROUP * D * 9 * TILE,
        scratch=[pltpu.VMEM((2, BLOCKS, FEED, TILE), BF16), pltpu.SemaphoreType.DMA((2,))] + loads_of(n, dg, du, act, gm),
        to_hbm=True,
    )[0]


def attention_grads_kernel(row, *refs):
    sources, (vec_ref, out_ref, held, sems), refs = refs[:6], refs[6:10], refs[10:]
    loads = Loads(sources, refs[:6], refs[6])
    copies = []
    n, dq, dk, dv = [ref[...] for ref in loads.wait(0, 3, 4, 5)]
    for b in range(BLOCKS):
        left = n[:, TILE * b : TILE * (b + 1)]
        for j, right in enumerate((dq, dk, dv)):
            half, at = divmod(TILE * j, ATTN)
            held[half, b, at : at + TILE, :] = dot_tn(left, right).astype(BF16)
    dattn, o = [ref[...] for ref in loads.wait(1, 2)]
    for j in range(BLOCKS):
        part = dot_tn(o, dattn[:, TILE * j : TILE * (j + 1)]).astype(BF16)
        held[1, :, TILE + 32 * j : TILE + 32 * (j + 1), :] = part.reshape(BLOCKS, 32, TILE)
    send_out(copies, held, out_ref.at[:, :, row : row + ATTN, :], sems.at[0])
    send_out(copies, vec_ref, out_ref.at[:, :, row + ATTN : row + ATTN + VEC, :], sems.at[1])
    for copy in copies:
        copy.wait()


def attention_grads(after, sums, n, dattn, o, dq, dk, dv, vec):
    return call(
        without(functools.partial(attention_grads_kernel, FEED + VEC), 0),
        (sums, n, dattn, o, dq, dk, dv, vec),
        [shape_of(2, BLOCKS, SUMS, TILE)],
        hbm=7,
        in_place=True,
        after=after,
        flops=2 * GROUP * D * 4 * TILE,
        scratch=[pltpu.VMEM((2, BLOCKS, ATTN, TILE), BF16), pltpu.SemaphoreType.DMA((2,))] + loads_of(n, dattn, o, dq, dk, dv),
        to_hbm=True,
    )[0]


def add_kernel(a_ref, b_ref, first_ref, *refs):
    for k, ref in enumerate((first_ref, *refs)):
        rows = slice(ROWS * k, ROWS * (k + 1))
        ref[...] = (a_ref[rows, :].astype(F32) + b_ref[rows, :].astype(F32)).astype(ref.dtype)


def added(after, a, b):
    return call(
        add_kernel,
        (a, b),
        [shape_of(ROWS, D, dtype=F32)] + [shape_of(ROWS, D)] * 3,
        flops=HALF * D,
        after=after,
    )


def total_of(refs):
    total = refs[0][...]
    for ref in refs[1:]:
        total = total + ref[...].astype(F32)
    return total


def unit_of(values):
    mean = jnp.mean(values, axis=-1, keepdims=True)
    centred = values - mean
    scale = lax.rsqrt(jnp.mean(centred * centred, axis=-1, keepdims=True) + EPSILON)
    return centred * scale, scale


def norm_kernel(row, base_ref, *refs):
    parts, (gain_ref, out_ref, n_ref) = refs[:4], refs[4:]
    out = (base_ref[...].astype(F32) + total_of(parts)).astype(out_ref.dtype)
    out_ref[...] = out
    unit, _ = unit_of(out.astype(F32))
    n_ref[...] = (unit * gain_ref[row : row + 1, :] + gain_ref[row + 1 : row + 2, :]).astype(BF16)


def normed(after, base, parts, gains, row, dtype):
    return call(
        functools.partial(norm_kernel, row),
        (base, *parts, gains),
        [shape_of(ROWS, D, dtype=dtype), shape_of(ROWS, D)],
        flops=16 * ROWS * D,
        after=after,
    )


def norm_back_kernel(row, up_ref, *refs):
    parts, (values_ref, gain_ref, grad_ref, low_ref, sum_ref) = refs[:4], refs[4:]
    e = total_of(parts)
    unit, scale = unit_of(values_ref[...].astype(F32))
    q = e * gain_ref[row : row + 1, :]
    back = scale * (q - jnp.mean(q, axis=-1, keepdims=True) - unit * jnp.mean(q * unit, axis=-1, keepdims=True))
    grad = up_ref[...].astype(F32) + back
    grad_ref[...] = grad
    low_ref[...] = grad.astype(BF16)
    sums = [jnp.sum(e * unit, axis=0, keepdims=True), jnp.sum(e, axis=0, keepdims=True)]
    sum_ref[...] = jnp.concatenate(sums + [jnp.zeros((6, D), F32)], axis=0)


def normed_back(after, up, parts, values, gains, row):
    return call(
        functools.partial(norm_back_kernel, row),
        (up, *parts, values, gains),
        [shape_of(ROWS, D, dtype=F32), shape_of(ROWS, D), shape_of(8, D, dtype=F32)],
        flops=32 * ROWS * D,
        after=after,
    )


def feed_both_kernel(w_ref, *refs):
    m_refs, n_refs = refs[:8], refs[8:16]
    pa_ref, pb_ref, ea_ref, eb_ref, *refs = refs[16:]
    held, sems, kept = refs[5], refs[6], Kept(refs[:5], (*refs[8:13], refs[13]))
    n_ref, m_ref, act_ref, dg_ref, du_ref = kept.held
    loads = Loads(m_refs, [m_ref.at[ROWS * k : ROWS * (k + 1), :] for k in range(8)], refs[7])
    first, last = feed_pieces()
    weights = Weights(w_ref, held, sems, last + first)
    n = rows_of(n_refs)
    n_ref[...] = n
    kept.send(0)
    loads.wait(*range(8))
    gm = m_ref[...]
    kept.send(1)
    weights.wait(0)
    weights.wait(1)
    for j in range(3):
        lanes = slice(TILE * j, TILE * (j + 1))
        weights.wait(2 + 2 * j)
        g = dot(n, weights.tile(TILE * j))
        weights.wait(3 + 2 * j)
        u = dot(n, weights.tile(TILE * (3 + j)))
        da = jnp.zeros((GROUP, TILE), F32)
        for b in range(BLOCKS):
            w = weights.tile(6 * TILE + PADDED * b, PADDED)[lanes]
            da += dot_nt(gm[:, TILE * b : TILE * (b + 1)], w)
        sigma = jax.nn.sigmoid(g)
        act_ref[:, lanes] = (g * sigma * u).astype(BF16)
        dg_ref[:, lanes] = (da * u * sigma * (1.0 + g * (1.0 - sigma))).astype(BF16)
        du_ref[:, lanes] = (da * g * sigma).astype(BF16)
    for k in range(2, 5):
        kept.send(k)
    act = act_ref[...]
    dg = dg_ref[...]
    du = du_ref[...]
    for b in range(BLOCKS):
        e = jnp.zeros((GROUP, TILE), F32)
        for j in range(3):
            lanes = slice(TILE * j, TILE * (j + 1))
            e += dot_nt(dg[:, lanes], weights.block(b, TILE * j))
            e += dot_nt(du[:, lanes], weights.block(b, TILE * (3 + j)))
        put_halves(ea_ref, eb_ref, b, e)
        put_halves(pa_ref, pb_ref, b, dot(act, weights.tile(6 * TILE + PADDED * b, PADDED)))
    kept.wait()


def feed_both(after, weights, blocks, top):
    return call(
        feed_both_kernel,
        (weights, *top, *blocks),
        [shape_of(HALF, D)] * 4 + [shape_of(GROUP, D)] * 2 + [shape_of(GROUP, WIDE)] * 3,
        hbm=9,
        stay=4,
        after=after,
        flops=4 * GROUP * D * 9 * TILE,
        scratch=[pltpu.VMEM(FEED_SCRATCH, BF16), pltpu.SemaphoreType.DMA((8,)), pltpu.SemaphoreType.DMA((8,))],
    )


def pieces_in_order():
    place = np.zeros((WIDE, 8 * PIECE), np.float32)
    for z in range(4):
        for c in range(2):
            for k in range(PIECE):
                place[(4 * c + z) * PADDED + k, (2 * z + c) * PIECE + k] = 1.0
    return jnp.asarray(place, BF16)


def values_in_order():
    place = np.zeros((TILE, TILE), np.float32)
    for head in range(4):
        for half in range(2):
            for k in range(32):
                place[(half * 4 + head) * 32 + k, (head * 2 + half) * 32 + k] = 1.0
    return jnp.asarray(place, BF16)


def columns_of(ref, b):
    return jnp.concatenate([ref[:, 64 * (8 * x + b) : 64 * (8 * x + b + 1)] for x in range(4)], axis=1)


def pack_rows_kernel(out_in, down_in, low_ref, high_ref, out_ref, down_ref, sems):
    Loads((out_in, down_in), (out_ref, down_ref), sems).wait(0, 1)
    pad = jnp.zeros((PADDED - PIECE, TILE), BF16)
    for b in range(BLOCKS):
        high_ref[32 * b : 32 * (b + 1), :] = columns_of(out_ref, b)
        down = jnp.concatenate([columns_of(down_ref, b), pad], axis=0)
        row = PADDED * (b % 4)
        if b < 4:
            low_ref[row : row + PADDED, :] = down
        else:
            high_ref[TILE + row : TILE + row + PADDED, :] = down
    low_ref[DOWN:, :] = jnp.zeros((TILE, TILE), BF16)


def packed_rows(out_weight, down_weight):
    return call(
        pack_rows_kernel,
        (out_weight, down_weight),
        [shape_of(DOWN + TILE, TILE), shape_of(DOWN + TILE, TILE)],
        hbm=2,
        scratch=loads_of(out_weight, down_weight),
        flops=1024,
    )


def pack_kernel(qkv_in, gate_in, places_in, values_in, cut_ref, *refs):
    loads = Loads((gate_in, places_in, qkv_in, values_in), refs[:4], refs[4])
    wide = 8 * PIECE
    gate_ref, places_ref = loads.wait(0, 1)
    rows = jnp.concatenate([gate_ref[:, wide * k : wide * (k + 1)] for k in range(16)], axis=0)
    placed = dot_nt(rows, places_ref[...]).astype(BF16)
    qkv_ref, values_ref = loads.wait(2, 3)
    values = jnp.concatenate([qkv_ref[:, 2 * D + TILE * t : 2 * D + TILE * (t + 1)] for t in range(8)], axis=0)
    values = dot_nt(values, values_ref[...]).astype(BF16)
    for t in range(8):
        cut_ref[0, t, 0] = qkv_ref[:, TILE * t : TILE * (t + 1)]
        cut_ref[0, t, 1] = qkv_ref[:, D + TILE * t : D + TILE * (t + 1)]
        cut_ref[1, t, 0] = values[32 * t : 32 * (t + 1)]
        cut_ref[1, t, 4] = jnp.zeros((32, TILE), BF16)
        for half in range(2):
            row = 32 * (8 * half + t)
            for j in range(3):
                cut_ref[half, t, 2 - half + j] = placed[row : row + 32, TILE * j : TILE * (j + 1)]


def packed(after, qkv_weight, gate_up):
    places, values = pieces_in_order(), values_in_order()
    return call(
        pack_kernel,
        (qkv_weight, gate_up, places, values),
        [shape_of(2, 8, 5, 32, TILE)],
        hbm=4,
        after=after,
        scratch=loads_of(gate_up, places, qkv_weight, values),
        flops=2 * 512 * WIDE * 8 * PIECE,
    )[0]


def put_columns(ref, blocks):
    for x in range(4):
        lanes = slice(64 * x, 64 * (x + 1))
        for k in range(4):
            pair = jnp.concatenate([blocks[2 * k][:, lanes], blocks[2 * k + 1][:, lanes]], axis=1)
            ref[:, 128 * (4 * x + k) : 128 * (4 * x + k + 1)] = pair.astype(F32)


def in_smem():
    return pl.BlockSpec(memory_space=pltpu.SMEM)


def to_owners_kernel(section_ref, sum_0, sum_1, cut_ref, kept_ref, sent_ref):
    lower = section_ref[0, 0] == 0
    rows = []
    for layer, ref in enumerate((sum_0, sum_1)):
        feed = [ref[TILE * j : TILE * (j + 1), :] for j in range(3)]
        down = ref[3 * TILE : FEED, :]
        attn = [ref[FEED + VEC + TILE * j : FEED + VEC + TILE * (j + 1), :] for j in range(2)]
        vecs = [ref[row : row + VEC, :].astype(F32) for row in (FEED + VEC + ATTN, FEED)]
        pad = jnp.zeros((30, TILE), F32)
        vec = [jnp.concatenate([v[o : o + 1] for v in vecs] + [pad], axis=0).astype(BF16) for o in range(8)]
        low = (attn[0], attn[1], feed[0], feed[1], feed[2])
        high = (attn[0], feed[0], feed[1], feed[2], jnp.concatenate(vec, axis=0))
        for t in range(5):
            tile = jnp.where(lower, low[t], high[t])
            for o in range(8):
                cut_ref[layer, o, t] = tile[32 * o : 32 * (o + 1)]
        rows.append((jnp.concatenate([down, attn[1]], axis=0), jnp.concatenate([attn[1], down], axis=0)))
    kept_ref[...] = jnp.where(lower, rows[0][0], rows[1][1])
    sent_ref[...] = jnp.where(lower, rows[1][0], rows[0][1])


def to_owners(after, section, sum_0, sum_1):
    kernel = to_owners_kernel
    for _ in after:
        kernel = without(kernel, 3)
    return pl.pallas_call(
        kernel,
        in_specs=[in_smem(), in_vmem(), in_vmem()] + [in_hbm()] * len(after),
        out_specs=[in_vmem()] * 3,
        out_shape=[shape_of(2, 8, 5, 32, TILE), shape_of(DOWN + TILE, TILE), shape_of(DOWN + TILE, TILE)],
        compiler_params=pltpu.CompilerParams(vmem_limit_bytes=VMEM),
    )(section, sum_0, sum_1, *(pltpu.with_memory_space_constraint(a, pltpu.HBM) for a in after))


def unpack_kernel(section_ref, kept_ref, sent_ref, places_ref, values_ref, cut_ref, qkv_ref, gate_ref, out_ref, down_ref, vec_ref):
    lower = section_ref[0, 0] == 0
    first = jnp.where(lower, kept_ref[:DOWN, :], sent_ref[:DOWN, :])
    second = jnp.where(lower, sent_ref[...], kept_ref[...])
    put_columns(out_ref, [second[32 * b : 32 * (b + 1)] for b in range(BLOCKS)])
    down = []
    for b in range(BLOCKS):
        row = PADDED * (b % 4)
        part = first[row : row + PADDED] if b < 4 else second[TILE + row : TILE + row + PADDED]
        down.append(part.astype(F32)[:PIECE])
    put_columns(down_ref, down)
    wide = 8 * PIECE
    vec = jnp.zeros((8, TILE), F32)
    for t in range(8):
        qkv_ref[:, TILE * t : TILE * (t + 1)] = cut_ref[0, t, 0].astype(F32)
        qkv_ref[:, D + TILE * t : D + TILE * (t + 1)] = cut_ref[0, t, 1].astype(F32)
        qkv_ref[:, 2 * D + TILE * t : 2 * D + TILE * (t + 1)] = dot(cut_ref[1, t, 0], values_ref[...])
        vec += cut_ref[1, t, 4].astype(F32)[:8]
    vec_ref[...] = vec
    rows = [
        jnp.concatenate([cut_ref[half, t, 2 - half + j] for j in range(3)], axis=1) for half in range(2) for t in range(8)
    ]
    placed = dot(jnp.concatenate(rows, axis=0), places_ref[...])
    for k in range(16):
        gate_ref[:, wide * k : wide * (k + 1)] = placed[32 * k : 32 * (k + 1)]


def unpacked(section, kept, sent, cut):
    return pl.pallas_call(
        unpack_kernel,
        in_specs=[in_smem()] + [in_vmem()] * 5,
        out_specs=[in_vmem()] * 5,
        out_shape=[
            shape_of(32, 3 * D, dtype=F32),
            shape_of(32, 2 * FF, dtype=F32),
            shape_of(32, D, dtype=F32),
            shape_of(PIECE, D, dtype=F32),
            shape_of(8, TILE, dtype=F32),
        ],
        compiler_params=pltpu.CompilerParams(vmem_limit_bytes=VMEM),
    )(section, kept, sent, pieces_in_order(), values_in_order(), cut)


def turned(block, axis, step):
    n = math.prod(lax.axis_size(a) for a in (axis if isinstance(axis, tuple) else (axis,)))
    return lax.ppermute(block, axis, [(i, (i - step) % n) for i in range(n)])


def in_order(block, axis, n):
    ahead = jnp.stack([block] + [turned(block, axis, k) for k in range(1, n)])
    return jnp.roll(ahead, lax.axis_index(axis), axis=0)


def gathered_rows(block):
    own = [block] + [turned(block, "x", k) for k in range(1, 4)]
    return own + [turned(part, "core", 1) for part in own]


def gathered_beside(block, work):
    own = [turned(block, "x", k) for k in range(1, 4)]
    *own, work = lax.optimization_barrier((*own, work))
    own = [block, *own]
    return own + [turned(part, "core", 1) for part in own], work


def summed_parts(after, part_a, part_b):
    first, *rest = added(after, part_a, turned(part_b, "core", 1))
    return [first] + [turned(block, "x", -k) for k, block in enumerate(rest, 1)]


def swapped(block, step):
    pairs = []
    for k in range(2):
        for y in range(2):
            for c in range(2):
                pairs.append((4 * k + 2 * y + c, 4 * ((k + step) % 2) + 2 * c + y))
    return lax.ppermute(block, ("section", "y", "core"), pairs)


def spread(block):
    return lax.all_to_all(block, ("section", "x", "core"), 0, 0, tiled=True)


def scattered(array):
    array = array.reshape(16, -1, TILE)
    return lax.optimization_barrier(lax.psum_scatter(array, SPREAD, scatter_dimension=0, tiled=False))


def to_stored(rows):
    shape = rows.shape[:-1]
    k = len(shape)
    cut = rows.reshape(*shape, 4, 8, 64)
    return jnp.swapaxes(cut, k, k + 1).reshape(*shape, D)


def from_stored(rows):
    shape = rows.shape[:-1]
    k = len(shape)
    cut = rows.reshape(*shape, 8, 4, 64)
    return jnp.swapaxes(cut, k, k + 1).reshape(*shape, D)


def value_columns(cut):
    shape = cut.shape[:-1]
    k = len(shape)
    return jnp.swapaxes(cut.reshape(*shape, 4, 2, 32), k, k + 1).reshape(*shape, TILE)


def value_columns_back(cut):
    shape = cut.shape[:-1]
    k = len(shape)
    return jnp.swapaxes(cut.reshape(*shape, 2, 4, 32), k, k + 1).reshape(*shape, TILE)


def both_layers(qkv_weight, out_weight, gate_up, down_weight):
    section = lax.axis_index("section")
    low, high = packed_rows(out_weight, down_weight)
    cut = spread(packed(None, qkv_weight, gate_up).reshape(16, 5, 32, TILE))
    cut = cut.reshape(2, 8, 5, 32, TILE).transpose(0, 2, 1, 3, 4).reshape(2, 5 * TILE, TILE)
    kept = swapped(jnp.where(section == 0, low, high), 0)
    sent = swapped(jnp.where(section == 0, high, low), 1)
    parts = []
    for layer in range(2):
        rows = jnp.where(section == layer, kept, sent)
        low = jnp.concatenate([cut[layer], rows[:DOWN]], axis=0)
        high = jnp.concatenate([cut[layer, :TILE], rows[:TILE], cut[layer, TILE : 4 * TILE], rows[TILE:]], axis=0)
        parts.append(jnp.where(section == 0, low, high))
    return parts


def owned(after, sum_0, sum_1):
    section = lax.axis_index("section").reshape(1, 1)
    cut, kept, sent = to_owners(after, section, sum_0, sum_1)
    kept, sent = swapped(kept, 0), swapped(sent, 1)
    cut = spread(cut.reshape(16, 5, 32, TILE)).reshape(2, 8, 5, 32, TILE)
    return unpacked(section, kept, sent, cut)


def geometry(segments):
    groups = segments.reshape(GROUP // 128, 128)
    index = jnp.arange(128, dtype=jnp.int32)
    block = index // 32
    same = (groups[:, :, None] == groups[:, None, :]) & (block[None, :, None] == block[None, None, :])
    before = index[None, :] < index[:, None]
    places = jnp.sum(jnp.where(same & before, 1.0, 0.0), axis=-1).astype(F32).reshape(GROUP)
    inverse = 10000.0 ** (-(jnp.arange(ROT // 2).astype(F32) * 2.0 / ROT))
    theta = places[:, None] * inverse
    cosine, sine = jnp.cos(theta), jnp.sin(theta)
    rest = HEAD_DIM - ROT
    zero = jnp.zeros((GROUP, ROT // 2), F32)
    straight = jnp.concatenate([cosine, cosine, jnp.ones((GROUP, rest), F32)], axis=1)
    first = jnp.concatenate([-sine, zero, jnp.zeros((GROUP, rest), F32)], axis=1)
    second = jnp.concatenate([zero, sine, jnp.zeros((GROUP, rest), F32)], axis=1)
    table = jnp.stack([jnp.concatenate([t, t], axis=1) for t in (straight, first, second)])
    linked = same & (index[None, :] <= index[:, None])
    return table, jnp.where(linked, 1.0, 0.0).astype(F32).reshape(GROUP, 128)


def vector_rows(*parts):
    cut = jnp.concatenate(parts, axis=2).astype(BF16)
    cut = jnp.pad(cut, ((0, 0), (0, VEC - 8), (0, TILE - cut.shape[2])))
    return jnp.stack([jnp.zeros_like(cut), cut])


def by_owner(vector):
    return vector.reshape(8, 8, 32)


def on_device(
    block_input,
    segment_ids,
    cotangent,
    first_gain,
    first_shift,
    qkv_weight,
    qkv_bias,
    out_weight,
    second_gain,
    second_shift,
    gate_up,
    down_weight,
):
    section = lax.axis_index("section")
    shard = 2 * lax.axis_index("x") + lax.axis_index("core")

    weights = []
    for part in both_layers(qkv_weight[0], out_weight[0], gate_up[0], down_weight[0]):
        full = lax.all_gather(part, SPREAD, axis=0, tiled=True)
        weights.append(full.reshape(2, BLOCKS, LAYER, TILE))

    vectors = jnp.concatenate([first_gain[0], first_shift[0], second_gain[0], second_shift[0], qkv_bias[0]])
    vectors = jnp.pad(vectors, (0, 32)).reshape(1, TILE)
    vectors = in_order(vectors, "core", 2)
    vectors = in_order(vectors, "x", 4)
    vectors = in_order(vectors, "z", 4)
    vectors = in_order(vectors, RING, 4)
    vectors = vectors.reshape(2, 64, TILE).astype(F32)
    gains = vectors[:, :, :128].reshape(2, 64, 4, 32).transpose(0, 2, 1, 3).reshape(8, D)
    bias = vectors[:, :, 128:224].reshape(2, 2, 4, 4, 2, 96).transpose(0, 3, 1, 2, 4, 5).reshape(2, 3, 8, TILE)
    bias = lax.dynamic_index_in_dim(bias, shard, 2, keepdims=False)
    bias = jnp.concatenate([bias[:, :2], value_columns(bias[:, 2:])], axis=1)
    bias = jnp.pad(bias, ((0, 0), (0, 5), (0, 0)))

    def own_rows(array):
        return lax.dynamic_slice_in_dim(array, 2 * section, 2, 0)

    rows_in = to_stored(own_rows(block_input).reshape(ROWS, D))
    top_grad = to_stored(own_rows(cotangent).reshape(ROWS, D))
    segments = gathered_rows(own_rows(segment_ids).reshape(1, ROWS))
    tables = geometry(jnp.concatenate(segments, axis=0))
    top = gathered_rows(top_grad)
    outputs = [None, None]
    kept = [{}, {}]
    base = rows_in
    unit, _ = unit_of(base.astype(F32))
    n = (unit * gains[0:1] + gains[1:2]).astype(BF16)
    for layer in range(2):
        have = kept[layer]
        part_a, part_b, have["n1"], have["q"], have["k"], have["v"], have["mixed"] = attention(
            top if layer == 0 else None, weights[layer], gathered_rows(n), bias[layer], *tables
        )
        have["values1"] = base
        hidden, n = normed(None, base, summed_parts(None, part_a, part_b), gains, 4 * layer + 2, F32)
        have["values2"] = hidden
        if layer == 0:
            part_a, part_b, have["n2"], have["g"], have["u"], have["act"] = feed(None, weights[0], gathered_rows(n))
            base, n = normed(None, hidden, summed_parts(None, part_a, part_b), gains, 4, BF16)
            outputs[0] = base
    part_a, part_b, ea, eb, have["n2"], have["gm"], have["act"], have["dg"], have["du"] = feed_both(
        None, weights[1], gathered_rows(n), top
    )

    def feed_sums(have):
        sums = have["sums2"]
        vec = vector_rows(by_owner(sums[0]), by_owner(sums[1]))
        return feed_grads(None, have["n2"], have["dg"], have["du"], have["act"], have["gm"], vec)

    def attention_sums(have, buffer):
        sums = have["sums1"]
        bias_sum = have["bias_sum"]
        bias_sum = jnp.concatenate([bias_sum[:2], value_columns_back(bias_sum[2:3])], axis=0)
        bias_sum = lax.dynamic_update_slice_in_dim(jnp.zeros((3, 8, TILE), F32), bias_sum[:, None], shard, 1)
        bias_sum = bias_sum.reshape(4, 2, 4, 2, 96).transpose(1, 2, 0, 3, 4).reshape(8, 8, 96)
        vec = vector_rows(by_owner(sums[0]), by_owner(sums[1]), bias_sum)
        names = ("n1", "dattn", "mixed", "dq", "dk", "dv")
        return attention_grads(None, buffer, *(have[name] for name in names), vec)

    grads_in = [None, None]
    up = top_grad
    sums_1 = None
    for layer in (1, 0):
        have = kept[layer]
        if layer == 0:
            blocks, sums_1 = gathered_beside(up, sums_1)
            ea, eb, have["gm"], have["dg"], have["du"] = feed_back((sums_1,), weights[0], blocks, have["g"], have["u"])
        grad, low, have["sums2"] = normed_back(None, up, summed_parts(None, ea, eb), have["values2"], gains, 4 * layer + 2)
        blocks, buffer = gathered_beside(low, feed_sums(have))
        ea, eb, have["bias_sum"], have["dattn"], have["dq"], have["dk"], have["dv"] = attention_back(
            (buffer,), weights[layer], blocks, have["q"], have["k"], have["v"], *tables
        )
        parts = summed_parts(None, ea, eb)
        grads_in[layer], up, have["sums1"] = normed_back(None, grad, parts, have["values1"], gains, 4 * layer)
        if layer == 1:
            sums_1 = attention_sums(have, buffer)
    sums_0 = attention_sums(kept[0], buffer)
    first, *rest = summed_parts((sums_0,), part_a, part_b)
    total = kept[1]["values2"] + first
    for block in rest:
        total = total + block.astype(F32)
    outputs[1] = total.astype(BF16)

    sum_1 = scattered(sums_1)
    sum_0 = scattered(sums_0)
    def layer_rows(first, second):
        mine = jnp.where(section == 0, first, second)
        other = turned(jnp.where(section == 0, second, first).astype(BF16), "section", 1).astype(first.dtype)
        rows = jnp.where(section == 0, jnp.concatenate([mine, other]), jnp.concatenate([other, mine]))
        return from_stored(rows).reshape(1, 4, 32, D)

    activations = layer_rows(outputs[0], outputs[1])
    input_grads = layer_rows(grads_in[0], upstream_of(grads_in[1]))
    qkv_grad, gate_up_grad, out_grad, down_grad, small = owned((activations, input_grads), sum_0, sum_1)
    return (
        activations,
        input_grads,
        small[0][None, 0:32],
        small[0][None, 32:64],
        qkv_grad[None],
        small[0][None, 64:160],
        out_grad[None],
        small[1][None, 0:32],
        small[1][None, 32:64],
        gate_up_grad[None],
        down_grad[None],
    )


def upstream_of(grad_rows):
    return grad_rows.astype(BF16).astype(F32)


def solution(mesh):
    grid = Mesh(mesh.devices.reshape(2, 4, 2, 4, 2), GRID)
    return jax.shard_map(
        on_device,
        mesh=grid,
        in_specs=(
            P(None, DP, None),
            P(None, DP),
            P(None, DP, None),
            P("section", DP),
            P("section", DP),
            P("section", DP, None),
            P("section", DP),
            P("section", DP, None),
            P("section", DP),
            P("section", DP),
            P("section", DP, None),
            P("section", DP, None),
        ),
        out_specs=(
            P("section", None, DP, None),
            P("section", None, DP, None),
            P("section", DP),
            P("section", DP),
            P("section", DP, None),
            P("section", DP),
            P("section", DP, None),
            P("section", DP),
            P("section", DP),
            P("section", DP, None),
            P("section", DP, None),
        ),
        check_vma=False,
    )
```
